512 devices in a mesh: fsdp: 4 (over x), ctx: 16 (over z, core), ch: 8 (over y).
Axes of the slice: x: 4, y: 8, z: 8, core: 2. Of those that a mesh axis runs over, the one named last changes fastest.
Arguments:
- tokens: bfloat16 [16384, 4096], P(('fsdp', 'ctx'), 'ch'), may hold values from -6 to 6
- w_query: bfloat16 [4096, 2048], P(('fsdp', 'ctx'), 'ch'), may hold values from -0.09375 to 0.09375
- w_key: bfloat16 [4096, 2048], P(('fsdp', 'ctx'), 'ch'), may hold values from -0.09375 to 0.09375
- w_value: bfloat16 [4096, 2048], P(('fsdp', 'ctx'), 'ch'), may hold values from -0.09375 to 0.09375
- short_taps: float32 [3, 3, 2048], P(None, None, 'ch'), may hold values from -3 to 3
- long_filter: float32 [16384, 2048], P(('fsdp', 'ctx'), 'ch'), may hold values from -6 to 6
- filter_bias: float32 [2048], P('ch'), may hold values from -4 to 4
Outputs:
- mixed_out: bfloat16 [16384, 2048], P(('fsdp', 'ctx'), 'ch')
The draws below stay inside these ranges and needn't reach their ends.
All inputs are finite; a program needn't handle non-finite values.
Results may differ from the reference program's by a relative error of at most 0.0064.
Values may be sent and summed in bfloat16 or wider, within the bound.
A program may use at most 64 MiB of HBM per device.

```python
import math
import jax
import jax.numpy as jnp

D = 4096
C = 2048
SEQ = 16384


def draw_long_filter(key, part):
    key = jax.random.fold_in(key, 7)
    rate_key, body_key = jax.random.split(key, 2)
    lowest = math.log(40.0)
    highest = math.log(40.0 * SEQ)
    reach = jnp.exp(jax.random.uniform(rate_key, (C,), jnp.float32, lowest, highest))
    times = jnp.arange(SEQ, dtype=jnp.float32)[:, None]
    envelope = jnp.exp(-times / reach[None, :])
    energy = -jnp.expm1(-2.0 * SEQ / reach) / -jnp.expm1(-2.0 / reach)
    rough = jnp.clip(jax.random.normal(body_key, (SEQ, C), jnp.float32), -6.0, 6.0)
    return rough * envelope / jnp.sqrt(energy)[None, :]


def levels(key, dims, cuts, low, largest):
    loudness, own = 1.0, jax.random.fold_in(key, 6)
    for axis_at, shards_of in cuts:
        draws = jnp.exp(jax.random.uniform(jax.random.fold_in(own, axis_at), (shards_of,), jnp.float32, low / len(cuts), largest / len(cuts)))
        loudness = loudness * jnp.repeat(draws, dims[axis_at] // shards_of).reshape([-1 if axis == axis_at else 1 for axis in range(len(dims))])
    return loudness


def bell_draw(key, dims, spread, most, pieces=(), kind=jnp.bfloat16):
    gain = levels(key, dims, pieces, -0.22, 0.18) if pieces else 1.0
    array = jax.random.normal(key, dims, jnp.float32) * spread * gain
    return jnp.minimum(jnp.maximum(array, -most), most).astype(kind)


def setup_inputs(seed: int = 0) -> dict:
    seeds = jax.random.split(jax.random.key(seed), 8)
    return {
        "tokens": bell_draw(seeds[0], (SEQ, D), 1.0, 6.0, ((0, 64), (1, 8))),
        "w_query": bell_draw(seeds[1], (D, C), D ** -0.5, 0.09375, ((0, 64), (1, 8))),
        "w_key": bell_draw(seeds[2], (D, C), D ** -0.5, 0.09375, ((0, 64), (1, 8))),
        "w_value": bell_draw(seeds[3], (D, C), D ** -0.5, 0.09375, ((0, 64), (1, 8))),
        "short_taps": bell_draw(seeds[4], (3, 3, C), 0.6, 3.0, ((2, 8),), jnp.float32),
        "long_filter": draw_long_filter(jax.random.fold_in(seeds[7], 71), 0),
        "filter_bias": bell_draw(seeds[6], (C,), 1.0, 4.0, ((0, 8),), jnp.float32),
    }


def short_conv(stream, taps):
    values = stream.astype(jnp.float32)
    padded = jnp.pad(values, ((2, 0), (0, 0)))
    return taps[0] * values + taps[1] * padded[1:1 + SEQ] + taps[2] * padded[0:SEQ]


def reference(tokens, w_query, w_key, w_value, short_taps, long_filter, filter_bias):
    query = jnp.dot(tokens, w_query, preferred_element_type=jnp.float32).astype(jnp.bfloat16)
    key_proj = jnp.dot(tokens, w_key, preferred_element_type=jnp.float32).astype(jnp.bfloat16)
    value = jnp.dot(tokens, w_value, preferred_element_type=jnp.float32).astype(jnp.bfloat16)
    query_conv = short_conv(query, short_taps[0])
    key_conv = short_conv(key_proj, short_taps[1])
    value_conv = short_conv(value, short_taps[2])
    gated = key_conv * value_conv
    length = 2 * SEQ
    spectrum = jnp.fft.rfft(gated, n=length, axis=0) * jnp.fft.rfft(long_filter, n=length, axis=0)
    conv = jnp.fft.irfft(spectrum, n=length, axis=0)[:SEQ]
    return (query_conv * (conv + filter_bias[None, :] * gated)).astype(jnp.bfloat16)
```

```python
import jax
import jax.numpy as jnp
from jax import lax
from jax.experimental import pallas as pl
from jax.experimental.pallas import tpu as pltpu
from jax.sharding import PartitionSpec as P

MESH = pl.DeviceIdType.MESH
X, Z, Y = 4, 8, 8
CHIPS = X * Z
ROWS = 256
HALF = 128
POS = 2 * ROWS
KB = 512
BLK = 64
F32 = jnp.float32
BF16 = jnp.bfloat16
N_STATIC = 144


def kernel(
    tokens, w_q, w_k, w_v, taps, filt, bias, out,
    tok, wq, wkv, acc, sq, sk, sv, gated_s, qconv_s, halo, filt_s,
    stage, snd_h, rcv_h, snd_g, rcv_g, snd_y, rcv_y, flat, epad, windows, toep, ysum, obuf,
    loc_sem, ss, rs, ss_h, rs_h, ss_g, rs_g, ss_y, rs_y,
):
    x = lax.axis_index("fsdp")
    cx = lax.axis_index("ctx")
    y = lax.axis_index("ch")
    z = cx // 2
    k = cx % 2
    chip = x * Z + z

    def at(xx, zz, kk, yy):
        return (xx, zz * 2 + kk, yy)

    def xm(d):
        return lax.rem(x + d + X, X)

    def zm(d):
        return lax.rem(z + d + Z, Z)

    def ym(d):
        return lax.rem(y + d + Y, Y)

    sibling = at(x, z, 1 - k, y)
    x_to = {s: at(xm(s), z, k, y) for s in (1, -1)}
    z_to = {s: at(x, zm(s), k, y) for s in (1, -1)}
    y_to = {s: at(x, z, k, ym(s)) for s in (1, -1)}
    after = lax.rem(chip + 1, CHIPS)
    before = lax.rem(chip + CHIPS - 1, CHIPS)

    def peer(r):
        p = lax.rem(chip + r, CHIPS)
        return p, at(p // Z, p % Z, k, y)

    barrier = pltpu.get_barrier_semaphore()
    for target in (sibling, y_to[1], y_to[-1]):
        pl.semaphore_signal(barrier, inc=1, device_id=target, device_id_type=MESH)

    def greet(r, carry):
        _, target = peer(r)
        pl.semaphore_signal(barrier, inc=1, device_id=target, device_id_type=MESH)
        return carry

    lax.fori_loop(1, CHIPS, greet, 0)
    pl.semaphore_wait(barrier, CHIPS - 1 + 3)

    index = {}
    pending = []

    def send(name, src, dst, target):
        n = index.setdefault(name, len(index))
        copy = pltpu.make_async_remote_copy(
            src_ref=src, dst_ref=dst, send_sem=ss.at[n], recv_sem=rs.at[n],
            device_id=target, device_id_type=MESH)
        copy.start()
        pending.append(copy)

    def recv(name, dst):
        n = index[name]
        pltpu.make_async_remote_copy(
            src_ref=dst, dst_ref=dst, send_sem=ss.at[n], recv_sem=rs.at[n],
            device_id=sibling, device_id_type=MESH).wait_recv()

    mine = pl.ds(pl.multiple_of(k * HALF, HALF), HALF)
    theirs = pl.ds(pl.multiple_of((1 - k) * HALF, HALF), HALF)

    own_rows = pl.ds(pl.multiple_of(chip * 128 + k * 64, 64), 64)
    sib_rows = pl.ds(pl.multiple_of(chip * 128 + (1 - k) * 64, 64), 64)
    send("sq", w_q.at[:, theirs], wq.at[own_rows, :], sibling)
    send("sk", w_k.at[:, theirs], wkv.at[own_rows, 0:HALF], sibling)
    send("sv", w_v.at[:, theirs], wkv.at[own_rows, HALF:2 * HALF], sibling)
    local = [
        pltpu.make_async_copy(w_q.at[:, mine], wq.at[own_rows, :], loc_sem.at[0]),
        pltpu.make_async_copy(w_k.at[:, mine], wkv.at[own_rows, 0:HALF], loc_sem.at[1]),
        pltpu.make_async_copy(w_v.at[:, mine], wkv.at[own_rows, HALF:2 * HALF], loc_sem.at[2]),
    ]
    for copy in local:
        copy.start()

    def tok_half(block, h):
        return tok.at[k, block, h * 128:(h + 1) * 128, :]

    for h in (0, 1):
        for s in (1, -1):
            send(("t", s, 1, h), tokens.at[h * 128:(h + 1) * 128, :], tok_half(y, h), y_to[s])
    own_tok = pltpu.make_async_copy(tokens, tok.at[k, y], loc_sem.at[3])
    own_tok.start()
    send(("ts", 0), tokens, tok.at[k, y], sibling)
    my_lags = pl.ds(pl.multiple_of(k * ROWS, ROWS), ROWS)
    sib_lags = pl.ds(pl.multiple_of((1 - k) * ROWS, ROWS), ROWS)
    send("f", filt.at[:, theirs], filt_s.at[my_lags, :], sibling)
    own_filt = pltpu.make_async_copy(filt.at[:, mine], filt_s.at[my_lags, :], loc_sem.at[4])
    own_filt.start()

    def tok_recv(s, d, h):
        block = ym(-s * d)
        recv(("t", s, d, h), tok_half(block, h))
        if d < 3 or (d == 3 and h == (0 if s == 1 else 1)):
            send(("t", s, d + 1, h), tok_half(block, h), tok_half(block, h), y_to[s])
        if h == 1 and d < 4:
            send(("ts", -s * d), tok.at[k, block], tok.at[k, block], sibling)

    def wrows(xx, zz, half=None):
        base = (xx * Z + zz) * 128
        if half is None:
            return pl.ds(pl.multiple_of(base, 128), 128)
        return pl.ds(pl.multiple_of(base + 64 * half, 64), 64)

    def hop(buf, name, xx, zz, target, half=None):
        ref = buf.at[wrows(xx, zz, half), :]
        send(name, ref, ref, target)

    def got(buf, name, xx, zz, half=None):
        recv(name, buf.at[wrows(xx, zz, half), :])

    side = {1: 0, -1: 1}

    def send_ax(s):
        hop(wq, ("ax", s), x, z, x_to[s])

    def got_ax(s):
        got(wq, ("ax", s), xm(-s), z)

    def send_axx(s):
        hop(wq, ("axx", s), xm(-s), z, x_to[s], side[s])

    def got_axx(s):
        got(wq, ("axx", s), xm(-2 * s), z, side[s])

    def send_az(b, s, d):
        hop(wq, ("az", b, s, d), xm(b), zm(-s * (d - 1)), z_to[s], side[s] if d == 4 else None)

    def got_az(b, s, d):
        got(wq, ("az", b, s, d), xm(b), zm(-s * d), side[s] if d == 4 else None)

    def send_bz(s, d):
        hop(wkv, ("bz", s, d), x, zm(-s * (d - 1)), z_to[s], side[s] if d == 4 else None)

    def got_bz(s, d):
        got(wkv, ("bz", s, d), x, zm(-s * d), side[s] if d == 4 else None)

    def send_bx(m, s):
        hop(wkv, ("bx", m, s), x, zm(m), x_to[s])

    def got_bx(m, s):
        got(wkv, ("bx", m, s), xm(-s), zm(m))

    def send_bxx(m, s):
        hop(wkv, ("bxx", m, s), xm(-s), zm(m), x_to[s], side[s])

    def got_bxx(m, s):
        got(wkv, ("bxx", m, s), xm(-2 * s), zm(m), side[s])

    both = (1, -1)

    for copy in local:
        copy.wait()
    recv("sq", wq.at[sib_rows, :])
    recv("sk", wkv.at[sib_rows, 0:HALF])
    recv("sv", wkv.at[sib_rows, HALF:2 * HALF])
    for s in both:
        send_bz(s, 1)
        send_ax(s)
    for s in both:
        send_az(0, s, 1)
        send_bx(0, s)

    def exchange(snd, rcv, send_sems, recv_sems):
        def start(r, carry):
            p, target = peer(r)
            pltpu.make_async_remote_copy(
                src_ref=snd.at[p], dst_ref=rcv.at[chip], send_sem=send_sems.at[r],
                recv_sem=recv_sems.at[r], device_id=target, device_id_type=MESH).start()
            return carry

        lax.fori_loop(1, CHIPS, start, 0)
        rcv[chip] = snd[chip]

    def collect(snd, rcv, send_sems, recv_sems):
        def finish(r, carry):
            p, target = peer(r)
            q, _ = peer(CHIPS - r)
            pltpu.make_async_remote_copy(
                src_ref=snd.at[p], dst_ref=rcv.at[q], send_sem=send_sems.at[r],
                recv_sem=recv_sems.at[r], device_id=target, device_id_type=MESH).wait()
            return carry

        lax.fori_loop(1, CHIPS, finish, 0)

    own_filt.wait()
    recv("f", filt_s.at[sib_lags, :])
    row_i = lax.broadcasted_iota(jnp.int32, (HALF, HALF), 0)
    col_i = lax.broadcasted_iota(jnp.int32, (HALF, HALF), 1)
    flip = (row_i + col_i == HALF - 1).astype(BF16)
    for jj in range(4):
        block = filt_s[jj * 128:(jj + 1) * 128, :].T.astype(BF16)
        stage[pl.ds(jj, HALF, stride=4), :] = jnp.dot(block, flip, preferred_element_type=F32)
    snd_h[...] = stage[...].astype(BF16).reshape(CHIPS, 16, HALF)
    exchange(snd_h, rcv_h, ss_h, rs_h)

    for s in both:
        got_ax(s)
        send_az(-s, 1, 1)
        send_az(-s, -1, 1)
        send_axx(s)
    for s in both:
        got_bz(s, 1)
        send_bz(s, 2)
        send_bx(-s, 1)
        send_bx(-s, -1)
    for s in both:
        got_bx(0, s)
        send_bxx(0, s)
        got_az(0, s, 1)
        send_az(0, s, 2)
    own_tok.wait()
    for s in both:
        tok_recv(s, 1, 0)
    got_axx(1)
    got_axx(-1)
    for s in both:
        send_az(2, s, 1)
    for s in both:
        got_bz(s, 2)
        send_bz(s, 3)
        send_bx(-2 * s, 1)
        send_bx(-2 * s, -1)
    for s in both:
        tok_recv(s, 1, 1)
    for m in (1, -1):
        for s in both:
            got_bx(m, s)
            send_bxx(m, s)
            got_az(m, s, 1)
            send_az(m, s, 2)
    for s in both:
        got_az(0, s, 2)
        send_az(0, s, 3)
    for s in both:
        tok_recv(s, 2, 0)

    collect(snd_h, rcv_h, ss_h, rs_h)
    flat[0:16, :] = jnp.zeros((16, HALF), F32)
    flat[16:, :] = rcv_h[...].astype(F32).reshape(CHIPS * 16, HALF)

    lane = lax.broadcasted_iota(jnp.int32, (BLK, HALF), 1)
    sub = lax.broadcasted_iota(jnp.int32, (BLK, HALF), 0)
    keep = lane + (BLK - 1) - sub < HALF

    def shifted_rows(c, v):
        j = 127 - v
        row = 16 + (j // 4) * 16 + 4 * c + j % 4
        wide = jnp.broadcast_to(flat[pl.ds(row, 1), :], (BLK, HALF))
        return pltpu.roll(wide, HALF - BLK + 1, 1, stride=1, stride_axis=0)

    def build(c):
        def body(d1, later):
            for p in range(7, -1, -1):
                now = shifted_rows(c, (15 - d1) * 8 + p)
                toep[c, d1, :, p * 128:(p + 1) * 128] = jnp.where(keep, now, later).astype(BF16)
                later = now
            return later

        lax.fori_loop(0, 16, body, jnp.zeros((BLK, HALF), F32))

    for s in both:
        got_bz(s, 3)
        send_bz(s, 4)
        send_bx(-3 * s, 1)
        send_bx(-3 * s, -1)
    for s in both:
        got_az(2, s, 1)
        send_az(2, s, 2)
    for m in (1, -1):
        for s in both:
            got_az(m, s, 2)
            send_az(m, s, 3)
    for s in both:
        got_az(0, s, 3)
        send_az(0, s, 4)
    for m in (2, -2):
        for s in both:
            got_bx(m, s)
            send_bxx(m, s)
    for s in both:
        tok_recv(s, 2, 1)
    build(0)
    for s in both:
        got_bz(s, 4)
    send_bx(4, 1)
    send_bx(4, -1)
    for s in both:
        got_az(2, s, 2)
        send_az(2, s, 3)
    for m in (1, -1):
        for s in both:
            got_az(m, s, 3)
            send_az(m, s, 4)
    for m in (3, -3):
        for s in both:
            got_bx(m, s)
            send_bxx(m, s)
    for s in both:
        tok_recv(s, 3, 0)
    build(1)
    for s in both:
        got_az(2, s, 3)
        send_az(2, s, 4)
    for s in both:
        got_bx(4, s)
        send_bxx(4, s)
    for s in both:
        tok_recv(s, 3, 1)
    build(2)
    build(3)
    for s in both:
        for b in (0, 1, -1, 2):
            got_az(b, s, 4)
        for m in (0, 1, -1, 2, -2, 3, -3, 4):
            got_bxx(m, s)
    far = ym(4)

    acc[...] = jnp.zeros_like(acc)

    def project(block, half):
        rows = pl.ds(pl.multiple_of(block * KB, KB), KB)
        a = tok[half, block]
        at_rows = pl.ds(pl.multiple_of(half * ROWS, ROWS), ROWS)
        acc[at_rows, 0:HALF] += jnp.dot(a, wq[rows, :], preferred_element_type=F32)
        acc[at_rows, HALF:] += jnp.dot(a, wkv[rows, :], preferred_element_type=F32)

    project(y, k)
    recv(("ts", 0), tok.at[1 - k, y])
    project(y, 1 - k)
    for d in (1, 2, 3):
        for s in both:
            project(ym(-s * d), k)
            recv(("ts", -s * d), tok.at[1 - k, ym(-s * d)])
            project(ym(-s * d), 1 - k)
    tok_recv(1, 4, 0)
    tok_recv(-1, 4, 1)
    send(("ts", 4), tok.at[k, far], tok.at[k, far], sibling)
    project(far, k)
    recv(("ts", 4), tok.at[1 - k, far])
    project(far, 1 - k)

    first = pl.ds(0, 8)
    streams = (sq, sk, sv)
    for i in range(3):
        streams[i][8:, :] = acc[:, i * HALF:(i + 1) * HALF].astype(BF16).astype(F32)
        halo[i] = streams[i][POS:POS + 8, :]
    nxt = at(after // Z, after % Z, k, y)
    for i in range(3):
        send(("h", i), halo.at[i], streams[i].at[first, :], nxt)

    def tap(i, j):
        return jnp.where(k == 0, taps[i, j:j + 1, 0:HALF], taps[i, j:j + 1, HALF:])

    def filtered(i, start, size):
        s = streams[i]
        return (tap(i, 0) * s[8 + start:8 + start + size, :] + tap(i, 1) * s[7 + start:7 + start + size, :]
                + tap(i, 2) * s[6 + start:6 + start + size, :])

    for i in range(3):
        recv(("h", i), streams[i].at[first, :])

    @pl.when(chip == 0)
    def _():
        for i in range(3):
            streams[i][0:8, :] = jnp.zeros((8, HALF), F32)

    for jj in range(4):
        block = filtered(1, jj * 128, 128) * filtered(2, jj * 128, 128)
        gated_s[jj * 128:(jj + 1) * 128, :] = block
        stage[pl.ds(jj, HALF, stride=4), :] = block.T
    snd_g[...] = stage[...].astype(BF16).reshape(CHIPS, 16, HALF)
    exchange(snd_g, rcv_g, ss_g, rs_g)
    for jj in range(4):
        qconv_s[jj * 128:(jj + 1) * 128, :] = filtered(0, jj * 128, 128)
    collect(snd_g, rcv_g, ss_g, rs_g)

    flat[16:, :] = rcv_g[...].astype(F32).reshape(CHIPS * 16, HALF)
    epad[0:16, :] = jnp.zeros((16, HALF), F32)
    ysum[0:16, :] = jnp.zeros((16, HALF), F32)
    low = lax.broadcasted_iota(jnp.int32, (CHIPS, HALF), 1) < BLK
    for c in range(4):
        for jj in range(4):
            now = flat[pl.ds(16 + 4 * c + jj, CHIPS, stride=16), :]
            prev_at = 16 + 4 * c + jj - 1 if jj else 4 * c + 3
            prev = flat[pl.ds(prev_at, CHIPS, stride=16), :]
            epad[pl.ds(16 + 2 * jj + 1, CHIPS, stride=8), :] = now
            epad[pl.ds(16 + 2 * jj, CHIPS, stride=8), :] = pltpu.roll(jnp.where(low, now, prev), BLK, 1)
        for p in range(8):
            windows[:, p * 128:(p + 1) * 128] = epad[2 + 2 * p:2 + 2 * p + 256, :].astype(BF16)
        ysum[16:, :] = jnp.zeros((256, HALF), F32)
        for u in range(4):
            count = 256 - 64 * u
            part = lax.dot_general(
                windows[0:count, :], toep[c, 4 * u:4 * u + 4].reshape(4 * BLK, 1024),
                (((1,), (1,)), ((), ())), preferred_element_type=F32)
            for w in range(2):
                d = 64 * u + 32 * w
                ysum[16 + d:, :] += part[0:256 - d, w * 128:(w + 1) * 128]
        for jj in range(4):
            a = ysum[pl.ds(16 + 2 * jj, CHIPS, stride=8), :]
            b = ysum[pl.ds(2 * jj, CHIPS, stride=8), :]
            e = ysum[pl.ds(16 + 2 * jj + 1, CHIPS, stride=8), :]
            f = ysum[pl.ds(2 * jj + 1, CHIPS, stride=8), :]
            stage[pl.ds(4 * c + jj, CHIPS, stride=16), :] = jnp.where(low, a, f) + pltpu.roll(
                jnp.where(low, e, b), BLK, 1)
    snd_y[...] = stage[...].astype(BF16).reshape(CHIPS, 16, HALF)
    exchange(snd_y, rcv_y, ss_y, rs_y)
    collect(snd_y, rcv_y, ss_y, rs_y)

    stage[...] = rcv_y[...].astype(F32).reshape(CHIPS * 16, HALF)
    direct = jnp.where(k == 0, bias[:, 0:HALF], bias[:, HALF:])
    for jj in range(4):
        conv = stage[pl.ds(jj, HALF, stride=4), :].T
        at_rows = slice(jj * 128, (jj + 1) * 128)
        obuf[jj // 2, (jj % 2) * 128:(jj % 2 + 1) * 128, :] = (
            qconv_s[at_rows, :] * (conv + direct * gated_s[at_rows, :])).astype(BF16)
    send("o", obuf.at[1 - k], obuf.at[2], sibling)
    out[:, mine] = obuf[k]
    recv("o", obuf.at[2])
    out[:, theirs] = obuf[2]
    for copy in pending:
        copy.wait_send()


def on_device(tokens, w_query, w_key, w_value, short_taps, long_filter, filter_bias):
    any_spec = pl.BlockSpec(memory_space=pl.ANY)
    vmem = pl.BlockSpec(memory_space=pltpu.VMEM)
    dma = pltpu.SemaphoreType.DMA
    return pl.pallas_call(
        kernel,
        out_shape=jax.ShapeDtypeStruct((ROWS, 2 * HALF), BF16),
        in_specs=[any_spec, any_spec, any_spec, any_spec, vmem, any_spec, vmem],
        out_specs=vmem,
        scratch_shapes=[
            pltpu.VMEM((2, Y, ROWS, KB), BF16),
            pltpu.VMEM((Y * KB, HALF), BF16),
            pltpu.VMEM((Y * KB, 2 * HALF), BF16),
            pltpu.VMEM((POS, 3 * HALF), F32),
            pltpu.VMEM((POS + 8, HALF), F32),
            pltpu.VMEM((POS + 8, HALF), F32),
            pltpu.VMEM((POS + 8, HALF), F32),
            pltpu.VMEM((POS, HALF), F32),
            pltpu.VMEM((POS, HALF), F32),
            pltpu.VMEM((3, 8, HALF), F32),
            pltpu.VMEM((POS, HALF), F32),
            pltpu.VMEM((POS, HALF), F32),
            pltpu.VMEM((CHIPS, 16, HALF), BF16),
            pltpu.VMEM((CHIPS, 16, HALF), BF16),
            pltpu.VMEM((CHIPS, 16, HALF), BF16),
            pltpu.VMEM((CHIPS, 16, HALF), BF16),
            pltpu.VMEM((CHIPS, 16, HALF), BF16),
            pltpu.VMEM((CHIPS, 16, HALF), BF16),
            pltpu.VMEM((16 + POS, HALF), F32),
            pltpu.VMEM((16 + 256, HALF), F32),
            pltpu.VMEM((256, 1024), BF16),
            pltpu.VMEM((4, 16, BLK, 1024), BF16),
            pltpu.VMEM((16 + 256, HALF), F32),
            pltpu.VMEM((3, ROWS, HALF), BF16),
            dma((5,)),
            dma((N_STATIC,)),
            dma((N_STATIC,)),
            dma((CHIPS,)),
            dma((CHIPS,)),
            dma((CHIPS,)),
            dma((CHIPS,)),
            dma((CHIPS,)),
            dma((CHIPS,)),
        ],
        compiler_params=pltpu.CompilerParams(
            collective_id=0, has_side_effects=True, vmem_limit_bytes=48 * 1024 * 1024),
        name="hyena",
    )(tokens, w_query, w_key, w_value, short_taps, long_filter, filter_bias.reshape(1, -1))


def solution(mesh):
    return jax.shard_map(
        on_device,
        mesh=mesh,
        in_specs=(
            P(("fsdp", "ctx"), "ch"),
            P(("fsdp", "ctx"), "ch"),
            P(("fsdp", "ctx"), "ch"),
            P(("fsdp", "ctx"), "ch"),
            P(None, None, "ch"),
            P(("fsdp", "ctx"), "ch"),
            P("ch"),
        ),
        out_specs=P(("fsdp", "ctx"), "ch"),
        check_vma=False,
    )
```

```python
import jax
import jax.numpy as jnp
from jax import lax
from jax.experimental import pallas as pl
from jax.experimental.pallas import tpu as pltpu
from jax.sharding import PartitionSpec as P

MESH = pl.DeviceIdType.MESH
X, Z, Y = 4, 8, 8
CHIPS = X * Z
ROWS = 256
HALF = 128
POS = 2 * ROWS
KB = 512
BLK = 64
F32 = jnp.float32
BF16 = jnp.bfloat16
N_RECV = 96
N_SEND = 12


def kernel(
    tokens, w_q, w_k, w_v, taps_hbm, filt, bias_hbm, out,
    tok, wq, wkv, acc, sq, sk, sv, gated_s, qconv_s, halo, filt_s,
    stage, snd_h, rcv_h, snd_g, rcv_g, snd_y, rcv_y, flat, epad, windows, toep, ysum, obuf,
    taps_s, bias_s, loc_sem, ss, rs, ss_x, rs_x,
):
    x = lax.axis_index("fsdp")
    cx = lax.axis_index("ctx")
    y = lax.axis_index("ch")
    z = cx // 2
    k = cx % 2
    chip = x * Z + z

    def at(xx, zz, kk, yy):
        return (xx, zz * 2 + kk, yy)

    def xm(d):
        return lax.rem(x + d + X, X)

    def zm(d):
        return lax.rem(z + d + Z, Z)

    def ym(d):
        return lax.rem(y + d + Y, Y)

    sibling = at(x, z, 1 - k, y)
    x_to = {s: at(xm(s), z, k, y) for s in (1, -1)}
    z_to = {s: at(x, zm(s), k, y) for s in (1, -1)}
    y_to = {s: at(x, z, k, ym(s)) for s in (1, -1)}
    after = lax.rem(chip + 1, CHIPS)
    before = lax.rem(chip + CHIPS - 1, CHIPS)

    def peer(r):
        p = lax.rem(chip + r, CHIPS)
        return p, at(p // Z, p % Z, k, y)

    barrier = pltpu.get_barrier_semaphore()
    for target in (sibling, y_to[1], y_to[-1]):
        pl.semaphore_signal(barrier, inc=1, device_id=target, device_id_type=MESH)

    def greet(r, carry):
        _, target = peer(r)
        pl.semaphore_signal(barrier, inc=1, device_id=target, device_id_type=MESH)
        return carry

    lax.fori_loop(1, CHIPS, greet, 0)
    pl.semaphore_wait(barrier, CHIPS - 1 + 3)

    arrivals, departures = {}, {}

    def send(name, src, dst, target, group):
        n = arrivals.setdefault(name, len(arrivals))
        g = departures.setdefault(group, len(departures))
        pltpu.make_async_remote_copy(
            src_ref=src, dst_ref=dst, send_sem=ss.at[g], recv_sem=rs.at[n],
            device_id=target, device_id_type=MESH).start()

    def recv(name, ref):
        pltpu.make_async_copy(ref, ref, rs.at[arrivals[name]]).wait()

    def sent(group, ref):
        pltpu.make_async_copy(ref, ref, ss.at[departures[group]]).wait()

    mine = pl.ds(pl.multiple_of(k * HALF, HALF), HALF)
    theirs = pl.ds(pl.multiple_of((1 - k) * HALF, HALF), HALF)

    own_rows = pl.ds(pl.multiple_of(chip * 128 + k * 64, 64), 64)
    sib_rows = pl.ds(pl.multiple_of(chip * 128 + (1 - k) * 64, 64), 64)
    send("sq", w_q.at[:, theirs], wq.at[own_rows, :], sibling, "sq")
    send("sk", w_k.at[:, theirs], wkv.at[own_rows, 0:HALF], sibling, "sk")
    send("sv", w_v.at[:, theirs], wkv.at[own_rows, HALF:2 * HALF], sibling, "sv")
    local = [
        pltpu.make_async_copy(w_q.at[:, mine], wq.at[own_rows, :], loc_sem.at[0]),
        pltpu.make_async_copy(w_k.at[:, mine], wkv.at[own_rows, 0:HALF], loc_sem.at[1]),
        pltpu.make_async_copy(w_v.at[:, mine], wkv.at[own_rows, HALF:2 * HALF], loc_sem.at[2]),
    ]
    for copy in local:
        copy.start()

    def tok_half(block, h):
        return tok.at[k, block, h * 128:(h + 1) * 128, :]

    for h in (0, 1):
        for s in (1, -1):
            send(("t", s, 1, h), tokens.at[h * 128:(h + 1) * 128, :], tok_half(y, h), y_to[s], "t")
    own_tok = pltpu.make_async_copy(tokens, tok.at[k, y], loc_sem.at[3])
    own_tok.start()
    send(("ts", 0), tokens, tok.at[k, y], sibling, "ts")
    my_lags = pl.ds(pl.multiple_of(k * ROWS, ROWS), ROWS)
    sib_lags = pl.ds(pl.multiple_of((1 - k) * ROWS, ROWS), ROWS)
    send("f", filt.at[:, theirs], filt_s.at[my_lags, :], sibling, "f")
    own_filt = pltpu.make_async_copy(filt.at[:, mine], filt_s.at[my_lags, :], loc_sem.at[4])
    own_filt.start()
    own_taps = pltpu.make_async_copy(taps_hbm, taps_s, loc_sem.at[5])
    own_taps.start()
    own_bias = pltpu.make_async_copy(bias_hbm, bias_s, loc_sem.at[6])
    own_bias.start()

    side = {1: 0, -1: 1}

    def tok_recv(s, d, h):
        block = ym(-s * d)
        recv(("t", s, d, h), tok_half(block, h))
        if d < 3:
            send(("t", s, d + 1, h), tok_half(block, h), tok_half(block, h), y_to[s], "t")
        elif h == side[s]:
            send(("t", 4), tok_half(block, h), tok_half(block, h), y_to[s], "t")
        if h == 1:
            send(("ts", -s * d), tok.at[k, block], tok.at[k, block], sibling, "ts")

    def wrows(xx, zz, half=None):
        base = (xx * Z + zz) * 128
        if half is None:
            return pl.ds(pl.multiple_of(base, 128), 128)
        return pl.ds(pl.multiple_of(base + 64 * half, 64), 64)

    def hop(buf, name, xx, zz, target, half=None):
        ref = buf.at[wrows(xx, zz, half), :]
        send(name, ref, ref, target, "wq" if buf is wq else "wkv")

    def got(buf, name, xx, zz):
        recv(name, buf.at[wrows(xx, zz), :])

    def send_ax(s):
        hop(wq, ("ax", s), x, z, x_to[s])

    def got_ax(s):
        got(wq, ("ax", s), xm(-s), z)

    def send_axx(s):
        hop(wq, "axx", xm(-s), z, x_to[s], side[s])

    def got_axx():
        got(wq, "axx", xm(2), z)

    def send_az(b, s, d):
        if d < 4:
            hop(wq, ("az", b, s, d), xm(b), zm(-s * (d - 1)), z_to[s])
        else:
            hop(wq, "azz", xm(b), zm(-s * 3), z_to[s], side[s])

    def got_az(b, s, d):
        got(wq, ("az", b, s, d), xm(b), zm(-s * d))

    def send_bz(s, d):
        if d < 4:
            hop(wkv, ("bz", s, d), x, zm(-s * (d - 1)), z_to[s])
        else:
            hop(wkv, "bzz", x, zm(-s * 3), z_to[s], side[s])

    def got_bz(s, d):
        got(wkv, ("bz", s, d), x, zm(-s * d))

    def got_bzz():
        got(wkv, "bzz", x, zm(4))

    def send_bx(m, s):
        hop(wkv, ("bx", m, s), x, zm(m), x_to[s])

    def got_bx(m, s):
        got(wkv, ("bx", m, s), xm(-s), zm(m))

    def send_bxx(m, s):
        hop(wkv, "bxx", xm(-s), zm(m), x_to[s], side[s])

    both = (1, -1)

    for copy in local:
        copy.wait()
    recv("sq", wq.at[sib_rows, :])
    recv("sk", wkv.at[sib_rows, 0:HALF])
    recv("sv", wkv.at[sib_rows, HALF:2 * HALF])
    for s in both:
        send_bz(s, 1)
        send_ax(s)
    for s in both:
        send_az(0, s, 1)
        send_bx(0, s)

    def exchange(snd, rcv, n):
        def start(r, carry):
            p, target = peer(r)
            pltpu.make_async_remote_copy(
                src_ref=snd.at[p], dst_ref=rcv.at[chip], send_sem=ss_x.at[n],
                recv_sem=rs_x.at[n], device_id=target, device_id_type=MESH).start()
            return carry

        lax.fori_loop(1, CHIPS, start, 0)
        rcv[chip] = snd[chip]

    def collect(rcv, n):
        all_but_one = rcv.at[0:CHIPS - 1]
        pltpu.make_async_copy(all_but_one, all_but_one, rs_x.at[n]).wait()

    def flushed(snd, n):
        all_but_one = snd.at[0:CHIPS - 1]
        pltpu.make_async_copy(all_but_one, all_but_one, ss_x.at[n]).wait()

    own_filt.wait()
    recv("f", filt_s.at[sib_lags, :])
    row_i = lax.broadcasted_iota(jnp.int32, (HALF, HALF), 0)
    col_i = lax.broadcasted_iota(jnp.int32, (HALF, HALF), 1)
    flip = (row_i + col_i == HALF - 1).astype(BF16)
    for jj in range(4):
        block = filt_s[jj * 128:(jj + 1) * 128, :].T.astype(BF16)
        stage[pl.ds(jj, HALF, stride=4), :] = jnp.dot(block, flip, preferred_element_type=F32)
    snd_h[...] = stage[...].astype(BF16).reshape(CHIPS, 16, HALF)
    exchange(snd_h, rcv_h, 0)

    for s in both:
        got_ax(s)
        send_az(-s, 1, 1)
        send_az(-s, -1, 1)
        send_axx(s)
    for s in both:
        got_bz(s, 1)
        send_bz(s, 2)
        send_bx(-s, 1)
        send_bx(-s, -1)
    for s in both:
        got_bx(0, s)
        send_bxx(0, s)
        got_az(0, s, 1)
        send_az(0, s, 2)
    own_tok.wait()
    for s in both:
        tok_recv(s, 1, 0)
    got_axx()
    for s in both:
        send_az(2, s, 1)
    for s in both:
        got_bz(s, 2)
        send_bz(s, 3)
        send_bx(-2 * s, 1)
        send_bx(-2 * s, -1)
    for s in both:
        tok_recv(s, 1, 1)
    for m in (1, -1):
        for s in both:
            got_bx(m, s)
            send_bxx(m, s)
            got_az(m, s, 1)
            send_az(m, s, 2)
    for s in both:
        got_az(0, s, 2)
        send_az(0, s, 3)
    for s in both:
        tok_recv(s, 2, 0)

    collect(rcv_h, 0)
    flat[0:16, :] = jnp.zeros((16, HALF), F32)
    flat[16:, :] = rcv_h[...].astype(F32).reshape(CHIPS * 16, HALF)

    lane = lax.broadcasted_iota(jnp.int32, (BLK, HALF), 1)
    sub = lax.broadcasted_iota(jnp.int32, (BLK, HALF), 0)
    keep = lane + (BLK - 1) - sub < HALF

    def shifted_rows(c, v):
        j = 127 - v
        row = 16 + (j // 4) * 16 + 4 * c + j % 4
        wide = jnp.broadcast_to(flat[pl.ds(row, 1), :], (BLK, HALF))
        return pltpu.roll(wide, HALF - BLK + 1, 1, stride=1, stride_axis=0)

    def build(c):
        def body(d1, later):
            for p in range(7, -1, -1):
                now = shifted_rows(c, (15 - d1) * 8 + p)
                toep[c, d1, :, p * 128:(p + 1) * 128] = jnp.where(keep, now, later).astype(BF16)
                later = now
            return later

        lax.fori_loop(0, 16, body, jnp.zeros((BLK, HALF), F32))

    for s in both:
        got_bz(s, 3)
        send_bz(s, 4)
        send_bx(-3 * s, 1)
        send_bx(-3 * s, -1)
    for s in both:
        got_az(2, s, 1)
        send_az(2, s, 2)
    for m in (1, -1):
        for s in both:
            got_az(m, s, 2)
            send_az(m, s, 3)
    for s in both:
        got_az(0, s, 3)
        send_az(0, s, 4)
    for m in (2, -2):
        for s in both:
            got_bx(m, s)
            send_bxx(m, s)
    for s in both:
        tok_recv(s, 2, 1)
    build(0)
    got_bzz()
    send_bx(4, 1)
    send_bx(4, -1)
    for s in both:
        got_az(2, s, 2)
        send_az(2, s, 3)
    for m in (1, -1):
        for s in both:
            got_az(m, s, 3)
            send_az(m, s, 4)
    for m in (3, -3):
        for s in both:
            got_bx(m, s)
            send_bxx(m, s)
    for s in both:
        tok_recv(s, 3, 0)
    build(1)
    for s in both:
        got_az(2, s, 3)
        send_az(2, s, 4)
    for s in both:
        got_bx(4, s)
        send_bxx(4, s)
    for s in both:
        tok_recv(s, 3, 1)
    build(2)
    build(3)
    recv("azz", wq.at[0:4 * 128, :])
    recv("bxx", wkv.at[0:8 * 128, :])
    far = ym(4)

    acc[...] = jnp.zeros_like(acc)

    def project(block, half):
        rows = pl.ds(pl.multiple_of(block * KB, KB), KB)
        a = tok[half, block]
        at_rows = pl.ds(pl.multiple_of(half * ROWS, ROWS), ROWS)
        acc[at_rows, 0:HALF] += jnp.dot(a, wq[rows, :], preferred_element_type=F32)
        acc[at_rows, HALF:] += jnp.dot(a, wkv[rows, :], preferred_element_type=F32)

    recv(("ts", 0), tok.at[1 - k, y])
    for d in (1, 2, 3):
        for s in both:
            recv(("ts", -s * d), tok.at[1 - k, ym(-s * d)])

    def near(t, carry):
        block = ym((t + 1) // 2 * (1 - 2 * (t % 2)))
        project(block, 0)
        project(block, 1)
        return carry

    lax.fori_loop(0, 7, near, 0)
    recv(("t", 4), tok.at[k, far])
    send(("ts", 4), tok.at[k, far], tok.at[k, far], sibling, "ts")
    project(far, k)
    recv(("ts", 4), tok.at[1 - k, far])
    project(far, 1 - k)

    first = pl.ds(0, 8)
    streams = (sq, sk, sv)
    for i in range(3):
        streams[i][8:, :] = acc[:, i * HALF:(i + 1) * HALF].astype(BF16).astype(F32)
        halo[i] = streams[i][POS:POS + 8, :]
    nxt = at(after // Z, after % Z, k, y)
    for i in range(3):
        send(("h", i), halo.at[i], streams[i].at[first, :], nxt, "h")

    own_taps.wait()
    own_bias.wait()

    def tap(i, j):
        return jnp.where(k == 0, taps_s[i, j:j + 1, 0:HALF], taps_s[i, j:j + 1, HALF:])

    def filtered(i, start, size):
        s = streams[i]
        return (tap(i, 0) * s[8 + start:8 + start + size, :] + tap(i, 1) * s[7 + start:7 + start + size, :]
                + tap(i, 2) * s[6 + start:6 + start + size, :])

    for i in range(3):
        recv(("h", i), streams[i].at[first, :])

    @pl.when(chip == 0)
    def _():
        for i in range(3):
            streams[i][0:8, :] = jnp.zeros((8, HALF), F32)

    for jj in range(4):
        block = filtered(1, jj * 128, 128) * filtered(2, jj * 128, 128)
        gated_s[jj * 128:(jj + 1) * 128, :] = block
        stage[pl.ds(jj, HALF, stride=4), :] = block.T
    snd_g[...] = stage[...].astype(BF16).reshape(CHIPS, 16, HALF)
    exchange(snd_g, rcv_g, 1)
    for jj in range(4):
        qconv_s[jj * 128:(jj + 1) * 128, :] = filtered(0, jj * 128, 128)
    collect(rcv_g, 1)

    flat[16:, :] = rcv_g[...].astype(F32).reshape(CHIPS * 16, HALF)
    epad[0:16, :] = jnp.zeros((16, HALF), F32)
    ysum[0:16, :] = jnp.zeros((16, HALF), F32)
    low = lax.broadcasted_iota(jnp.int32, (CHIPS, HALF), 1) < BLK
    for c in range(4):
        for jj in range(4):
            now = flat[pl.ds(16 + 4 * c + jj, CHIPS, stride=16), :]
            prev_at = 16 + 4 * c + jj - 1 if jj else 4 * c + 3
            prev = flat[pl.ds(prev_at, CHIPS, stride=16), :]
            epad[pl.ds(16 + 2 * jj + 1, CHIPS, stride=8), :] = now
            epad[pl.ds(16 + 2 * jj, CHIPS, stride=8), :] = pltpu.roll(jnp.where(low, now, prev), BLK, 1)
        for p in range(8):
            windows[:, p * 128:(p + 1) * 128] = epad[2 + 2 * p:2 + 2 * p + 256, :].astype(BF16)
        ysum[16:, :] = jnp.zeros((256, HALF), F32)
        for u in range(4):
            count = 256 - 64 * u
            part = lax.dot_general(
                windows[0:count, :], toep[c, 4 * u:4 * u + 4].reshape(4 * BLK, 1024),
                (((1,), (1,)), ((), ())), preferred_element_type=F32)
            for w in range(2):
                d = 64 * u + 32 * w
                ysum[16 + d:, :] += part[0:256 - d, w * 128:(w + 1) * 128]
        for jj in range(4):
            a = ysum[pl.ds(16 + 2 * jj, CHIPS, stride=8), :]
            b = ysum[pl.ds(2 * jj, CHIPS, stride=8), :]
            e = ysum[pl.ds(16 + 2 * jj + 1, CHIPS, stride=8), :]
            f = ysum[pl.ds(2 * jj + 1, CHIPS, stride=8), :]
            stage[pl.ds(4 * c + jj, CHIPS, stride=16), :] = jnp.where(low, a, f) + pltpu.roll(
                jnp.where(low, e, b), BLK, 1)
    snd_y[...] = stage[...].astype(BF16).reshape(CHIPS, 16, HALF)
    exchange(snd_y, rcv_y, 2)
    collect(rcv_y, 2)

    stage[...] = rcv_y[...].astype(F32).reshape(CHIPS * 16, HALF)
    direct = jnp.where(k == 0, bias_s[:, 0:HALF], bias_s[:, HALF:])
    for jj in range(4):
        conv = stage[pl.ds(jj, HALF, stride=4), :].T
        at_rows = slice(jj * 128, (jj + 1) * 128)
        obuf[jj // 2, (jj % 2) * 128:(jj % 2 + 1) * 128, :] = (
            qconv_s[at_rows, :] * (conv + direct * gated_s[at_rows, :])).astype(BF16)
    send("o", obuf.at[1 - k], out.at[:, mine], sibling, "o")
    final = pltpu.make_async_copy(obuf.at[k], out.at[:, mine], loc_sem.at[0])
    final.start()
    sent("sq", w_q.at[:, theirs])
    sent("sk", w_k.at[:, theirs])
    sent("sv", w_v.at[:, theirs])
    sent("f", filt.at[:, theirs])
    sent("t", tok.at[0, 0:7])
    sent("ts", tok.at[0])
    sent("wq", wq.at[0:31 * 128, :])
    sent("wkv", wkv.at[0:31 * 128, :])
    sent("h", halo)
    for n, snd in enumerate((snd_h, snd_g, snd_y)):
        flushed(snd, n)
    final.wait()
    sent("o", obuf.at[1 - k])
    recv("o", out.at[:, theirs])


def on_device(tokens, w_query, w_key, w_value, short_taps, long_filter, filter_bias):
    hbm = pl.BlockSpec(memory_space=pltpu.HBM)
    dma = pltpu.SemaphoreType.DMA
    return pl.pallas_call(
        kernel,
        out_shape=jax.ShapeDtypeStruct((ROWS, 2 * HALF), BF16),
        in_specs=[hbm] * 7,
        out_specs=hbm,
        scratch_shapes=[
            pltpu.VMEM((2, Y, ROWS, KB), BF16),
            pltpu.VMEM((Y * KB, HALF), BF16),
            pltpu.VMEM((Y * KB, 2 * HALF), BF16),
            pltpu.VMEM((POS, 3 * HALF), F32),
            pltpu.VMEM((POS + 8, HALF), F32),
            pltpu.VMEM((POS + 8, HALF), F32),
            pltpu.VMEM((POS + 8, HALF), F32),
            pltpu.VMEM((POS, HALF), F32),
            pltpu.VMEM((POS, HALF), F32),
            pltpu.VMEM((3, 8, HALF), F32),
            pltpu.VMEM((POS, HALF), F32),
            pltpu.VMEM((POS, HALF), F32),
            pltpu.VMEM((CHIPS, 16, HALF), BF16),
            pltpu.VMEM((CHIPS, 16, HALF), BF16),
            pltpu.VMEM((CHIPS, 16, HALF), BF16),
            pltpu.VMEM((CHIPS, 16, HALF), BF16),
            pltpu.VMEM((CHIPS, 16, HALF), BF16),
            pltpu.VMEM((CHIPS, 16, HALF), BF16),
            pltpu.VMEM((16 + POS, HALF), F32),
            pltpu.VMEM((16 + 256, HALF), F32),
            pltpu.VMEM((256, 1024), BF16),
            pltpu.VMEM((4, 16, BLK, 1024), BF16),
            pltpu.VMEM((16 + 256, HALF), F32),
            pltpu.VMEM((2, ROWS, HALF), BF16),
            pltpu.VMEM((3, 3, 2 * HALF), F32),
            pltpu.VMEM((1, 2 * HALF), F32),
            dma((7,)),
            dma((N_SEND,)),
            dma((N_RECV,)),
            dma((3,)),
            dma((3,)),
        ],
        compiler_params=pltpu.CompilerParams(
            collective_id=0, has_side_effects=True, vmem_limit_bytes=60 * 1024 * 1024),
        name="hyena",
    )(tokens, w_query, w_key, w_value, short_taps, long_filter, filter_bias.reshape(1, -1))


def solution(mesh):
    return jax.shard_map(
        on_device,
        mesh=mesh,
        in_specs=(
            P(("fsdp", "ctx"), "ch"),
            P(("fsdp", "ctx"), "ch"),
            P(("fsdp", "ctx"), "ch"),
            P(("fsdp", "ctx"), "ch"),
            P(None, None, "ch"),
            P(("fsdp", "ctx"), "ch"),
            P("ch"),
        ),
        out_specs=P(("fsdp", "ctx"), "ch"),
        check_vma=False,
    )
```

```python
import jax
import jax.numpy as jnp
from jax import lax
from jax.experimental import pallas as pl
from jax.experimental.pallas import tpu as pltpu
from jax.sharding import PartitionSpec as P

MESH = pl.DeviceIdType.MESH
X, Z, Y = 4, 8, 8
CHIPS = X * Z
ROWS = 256
HALF = 128
LEAD = 16
POS = 2 * ROWS
KB = 512
BLK = 64
F32 = jnp.float32
BF16 = jnp.bfloat16
N_RECV = 48
N_SEND = 12


def kernel(
    tokens, w_q, w_k, w_v, taps_hbm, filt, bias_hbm, out,
    tok, wq, wkv, acc, sq, sk, sv, gated_s, qconv_s, filt_s,
    stage, snd_h, rcv_h, snd_g, rcv_g, snd_y, rcv_y, flat, epad, windows, toep, ysum, obuf,
    taps_s, bias_s, loc_sem, ss, rs, ss_x, rs_x,
):
    x = lax.axis_index("fsdp")
    cx = lax.axis_index("ctx")
    y = lax.axis_index("ch")
    z = lax.div(cx, 2)
    k = lax.rem(cx, 2)
    chip = x * Z + z

    def at(xx, zz, kk, yy):
        return (xx, zz * 2 + kk, yy)

    def xm(d):
        return lax.rem(x + d + X, X)

    def zm(d):
        return lax.rem(z + d + Z, Z)

    def ym(d):
        return lax.rem(y + d + Y, Y)

    sibling = at(x, z, 1 - k, y)
    x_to = {s: at(xm(s), z, k, y) for s in (1, -1, 2)}
    z_to = {s: at(x, zm(s), k, y) for s in (1, -1, 2, -2)}
    y_to = {s: at(x, z, k, ym(s)) for s in (1, -1)}

    def peer(r):
        p = lax.rem(chip + r, CHIPS)
        return p, at(lax.div(p, Z), lax.rem(p, Z), k, y)

    barrier = pltpu.get_barrier_semaphore()
    x_across = {s: at(xm(s), z, 1 - k, y) for s in (1, -1, 2)}
    z_across = {s: at(x, zm(s), 1 - k, y) for s in (1, -1, 2, -2)}
    previous = lax.rem(chip + CHIPS - 1, CHIPS)
    greeted = [sibling, at(lax.div(previous, Z), lax.rem(previous, Z), 1 - k, y)]
    greeted += [at(x, z, k, ym(d)) for d in range(1, Y)]
    greeted += list(x_across.values()) + list(z_across.values())
    for target in greeted:
        pl.semaphore_signal(barrier, inc=1, device_id=target, device_id_type=MESH)

    def greet(r, carry):
        _, target = peer(r)
        pl.semaphore_signal(barrier, inc=1, device_id=target, device_id_type=MESH)
        return carry

    lax.fori_loop(1, CHIPS, greet, 0)
    pl.semaphore_wait(barrier, CHIPS - 1 + len(greeted))

    arrivals, departures = {}, {}

    def send(name, src, dst, target, group):
        n = arrivals.setdefault(name, len(arrivals))
        g = departures.setdefault(group, len(departures))
        pltpu.make_async_remote_copy(
            src_ref=src, dst_ref=dst, send_sem=ss.at[g], recv_sem=rs.at[n],
            device_id=target, device_id_type=MESH).start()

    def recv(name, ref):
        pltpu.make_async_copy(ref, ref, rs.at[arrivals[name]]).wait()

    def sent(group, ref):
        pltpu.make_async_copy(ref, ref, ss.at[departures[group]]).wait()

    mine = pl.ds(pl.multiple_of(k * HALF, HALF), HALF)
    theirs = pl.ds(pl.multiple_of((1 - k) * HALF, HALF), HALF)

    own_rows = pl.ds(pl.multiple_of(chip * 128 + k * 64, 64), 64)
    sib_rows = pl.ds(pl.multiple_of(chip * 128 + (1 - k) * 64, 64), 64)
    my_lags = pl.ds(pl.multiple_of(k * ROWS, ROWS), ROWS)
    sib_lags = pl.ds(pl.multiple_of((1 - k) * ROWS, ROWS), ROWS)

    def tok_half(block, h):
        return tok.at[k, block, LEAD + h * 128:LEAD + (h + 1) * 128, :]

    def tok_all(half, block):
        return tok.at[half, block, LEAD:, :]

    quarter = pl.ds(pl.multiple_of(k * 256, 256), 256)
    nxt = lax.rem(chip + 1, CHIPS)

    def send_lead():
        @pl.when(k == 1)
        def _():
            for kk in (0, 1):
                cut = pl.ds(kk * 256, 256)
                send("lead", tokens.at[ROWS - LEAD:, cut], tok.at[0, y, 0:LEAD, cut],
                     at(lax.div(nxt, Z), lax.rem(nxt, Z), kk, y), "lead")

    def spread_lead():
        ref = tok.at[0, y, 0:LEAD, quarter]
        recv("lead", ref)
        for d in range(1, Y):
            send("leads", ref, ref, at(x, z, k, ym(d)), "leads")

    def share_lead():
        recv("leads", tok.at[0, 0:7, 0:LEAD, quarter])
        ref = tok.at[0, :, 0:LEAD, quarter]
        send("leadx", ref, ref, sibling, "leadx")

    def got_lead():
        recv("leadx", tok.at[0, :, 0:LEAD, quarter])

    both = (1, -1)
    side = {1: 0, -1: 1}

    def tok_recv(d, h):
        recv(("t", d, h), tok_all(0, 0))
        for s in (1, -1):
            block = ym(-s * d)
            half_block = tok_half(block, h)
            if d < 3:
                send(("t", d + 1, h), half_block, half_block, y_to[s], "t")
            elif h == side[s]:
                send(("t", 4), half_block, half_block, y_to[s], "t")
            if h == 1:
                send(("ts", d), tok_all(k, block), tok_all(k, block), sibling, "ts")

    def wrows(xx, zz, half=None):
        base = (xx * Z + zz) * 128
        if half is None:
            return pl.ds(pl.multiple_of(base, 128), 128)
        return pl.ds(pl.multiple_of(base + 64 * half, 64), 64)

    def hop(buf, name, xx, zz, target, half=None):
        ref = buf.at[wrows(xx, zz, half), :]
        send(name, ref, ref, target, "wq" if buf is wq else "wkv")

    def got(buf, name, blocks=2):
        recv(name, buf.at[0:128 * blocks, :])


    def first_hop(buf, name, steps, near, across):
        for s in steps:
            for columns, target in ((mine, near[s]), (theirs, across[s])):
                if buf is wq:
                    send(name, w_q.at[:, columns], wq.at[own_rows, :], target, "wq")
                else:
                    send(name, w_k.at[:, columns], wkv.at[own_rows, 0:HALF], target, "wkv")
                    send(name, w_v.at[:, columns], wkv.at[own_rows, HALF:2 * HALF], target, "wkv")

    def pass_ax():
        got(wq, "ax")
        for s in both:
            for b in both:
                hop(wq, ("az", 1, 1), xm(b), z, z_to[s])

    def pass_axx():
        got(wq, "axx", 1)
        for s in both:
            hop(wq, ("az", 2, 1), xm(2), z, z_to[s])

    def pass_az(b, d):
        columns = both if b == 1 else (b,)
        got(wq, ("az", b, d), 2 * len(columns))
        for col in columns:
            for s in both:
                hop(wq, ("az", b, d + 1), xm(col), zm(-s * d), z_to[s], side[s] if d == 3 else None)

    def pass_bz(d):
        got(wkv, ("bz", d))
        if d > 1:
            for s in both:
                hop(wkv, ("bz", d + 1), x, zm(-s * d), z_to[s], side[s] if d == 3 else None)
        for s in both:
            for m in (d, -d):
                hop(wkv, ("bx", d), x, zm(m), x_to[s])

    def pass_bz4():
        got(wkv, ("bz", 4), 1)
        for s in both:
            hop(wkv, ("bx", 4), x, zm(4), x_to[s])

    def pass_bx(d):
        rows = (0,) if d == 0 else (4,) if d == 4 else (d, -d)
        got(wkv, ("bx", d), 2 * len(rows))
        for m in rows:
            for s in both:
                hop(wkv, "bxx", xm(-s), zm(m), x_to[s], side[s])

    send_lead()
    for h in (0, 1):
        for s in (1, -1):
            send(("t", 1, h), tokens.at[h * 128:(h + 1) * 128, :], tok_half(y, h), y_to[s], "t")
    first_hop(wkv, ("bz", 1), both, z_to, z_across)
    first_hop(wq, "ax", both, x_to, x_across)
    first_hop(wkv, ("bz", 2), (2, -2), z_to, z_across)
    first_hop(wq, "axx", (2,), x_to, x_across)
    first_hop(wkv, ("bx", 0), both, x_to, x_across)
    first_hop(wq, ("az", 0, 1), both, z_to, z_across)
    send("sq", w_q.at[:, theirs], wq.at[own_rows, :], sibling, "sq")
    send("sk", w_k.at[:, theirs], wkv.at[own_rows, 0:HALF], sibling, "sk")
    send("sv", w_v.at[:, theirs], wkv.at[own_rows, HALF:2 * HALF], sibling, "sv")
    local = [
        pltpu.make_async_copy(w_q.at[:, mine], wq.at[own_rows, :], loc_sem.at[0]),
        pltpu.make_async_copy(w_k.at[:, mine], wkv.at[own_rows, 0:HALF], loc_sem.at[1]),
        pltpu.make_async_copy(w_v.at[:, mine], wkv.at[own_rows, HALF:2 * HALF], loc_sem.at[2]),
    ]
    for copy in local:
        copy.start()

    own_tok = pltpu.make_async_copy(tokens, tok_all(k, y), loc_sem.at[3])
    own_tok.start()
    send(("ts", 0), tokens, tok_all(k, y), sibling, "ts")
    send("f", filt.at[:, theirs], filt_s.at[my_lags, :], sibling, "f")
    own_filt = pltpu.make_async_copy(filt.at[:, mine], filt_s.at[my_lags, :], loc_sem.at[4])
    own_filt.start()
    own_taps = pltpu.make_async_copy(taps_hbm, taps_s, loc_sem.at[5])
    own_taps.start()
    own_bias = pltpu.make_async_copy(bias_hbm, bias_s, loc_sem.at[6])
    own_bias.start()


    offsets = sorted(
        ((dx, dz) for dx in range(X) for dz in range(Z) if dx or dz),
        key=lambda o: -min(o[0], X - o[0]) - min(o[1], Z - o[1]))

    def exchange(snd, rcv, n):
        for dx, dz in offsets:
            px, pz = xm(dx), zm(dz)
            pltpu.make_async_remote_copy(
                src_ref=snd.at[px * Z + pz], dst_ref=rcv.at[chip], send_sem=ss_x.at[n],
                recv_sem=rs_x.at[n], device_id=at(px, pz, k, y), device_id_type=MESH).start()
        rcv[chip] = snd[chip]

    def collect(rcv, n):
        all_but_one = rcv.at[0:CHIPS - 1]
        pltpu.make_async_copy(all_but_one, all_but_one, rs_x.at[n]).wait()

    def flushed(snd, n):
        all_but_one = snd.at[0:CHIPS - 1]
        pltpu.make_async_copy(all_but_one, all_but_one, ss_x.at[n]).wait()

    def send_filter():
        own_filt.wait()
        recv("f", filt_s.at[sib_lags, :])
        row_i = lax.broadcasted_iota(jnp.int32, (HALF, HALF), 0)
        col_i = lax.broadcasted_iota(jnp.int32, (HALF, HALF), 1)
        flip = (row_i + col_i == HALF - 1).astype(BF16)
        for jj in range(4):
            block = filt_s[jj * 128:(jj + 1) * 128, :].T.astype(BF16)
            stage[pl.ds(jj, HALF, stride=4), :] = jnp.dot(block, flip, preferred_element_type=F32)
        snd_h[...] = stage[...].astype(BF16).reshape(CHIPS, 16, HALF)
        exchange(snd_h, rcv_h, 0)

    def got_filter():
        collect(rcv_h, 0)
        flat[0:16, :] = jnp.zeros((16, HALF), F32)
        flat[16:, :] = rcv_h[...].astype(F32).reshape(CHIPS * 16, HALF)

    lane = lax.broadcasted_iota(jnp.int32, (BLK, HALF), 1)
    sub = lax.broadcasted_iota(jnp.int32, (BLK, HALF), 0)
    keep = lane + (BLK - 1) - sub < HALF

    def shifted_rows(c, v):
        j = 127 - v
        row = 16 + (j // 4) * 16 + 4 * c + j % 4
        wide = jnp.broadcast_to(flat[pl.ds(row, 1), :], (BLK, HALF))
        return pltpu.roll(wide, HALF - BLK + 1, 1, stride=1, stride_axis=0)

    def build(piece):
        c, first = piece // 2, piece % 2 * 8

        def body(d1, later):
            for p in range(7, -1, -1):
                now = shifted_rows(c, (15 - d1) * 8 + p)
                toep[c, d1, :, p * 128:(p + 1) * 128] = jnp.where(keep, now, later).astype(BF16)
                later = now
            return later

        carried = jnp.zeros((BLK, HALF), F32) if first == 0 else shifted_rows(c, (16 - first) * 8)
        lax.fori_loop(first, first + 8, body, carried)

    def project(block, half):
        rows = pl.ds(pl.multiple_of(block * KB, KB), KB)
        if half == 0:
            a, at_rows = tok[0, block], slice(0, LEAD + ROWS)
        else:
            a, at_rows = tok[1, block, LEAD:, :], slice(LEAD + ROWS, LEAD + POS)
        acc[at_rows, 0:HALF] += jnp.dot(a, wq[rows, :], preferred_element_type=F32)
        acc[at_rows, HALF:] += jnp.dot(a, wkv[rows, :], preferred_element_type=F32)

    far = ym(4)

    def project_column(first, count):
        def body(t, carry):
            block = 2 * xm(first + 2 * lax.div(t, 2)) + lax.rem(t, 2)

            @pl.when(block != far)
            def _():
                project(block, 0)
                project(block, 1)

            return carry

        lax.fori_loop(0, 2 * count, body, 0)

    acc[...] = jnp.zeros_like(acc)
    spread_lead()
    pass_ax()
    pass_bz(1)
    tok_recv(1, 0)
    got(wq, "axx", 1)
    for s in both:
        hop(wq, ("az", 2, 1), xm(2), z, z_to[s])
    pass_bz(2)
    pass_bx(0)
    pass_az(0, 1)
    tok_recv(1, 1)
    send_filter()
    pass_az(1, 1)
    pass_bx(1)
    pass_az(2, 1)
    tok_recv(2, 0)
    share_lead()
    pass_bx(2)
    pass_bz(3)
    pass_az(0, 2)
    got_filter()
    build(0)
    tok_recv(2, 1)
    pass_az(1, 2)
    build(1)
    pass_az(2, 2)
    pass_bz4()
    pass_az(0, 3)
    build(2)
    tok_recv(3, 0)
    pass_bx(3)
    pass_az(1, 3)
    build(3)
    pass_bx(4)
    pass_az(2, 3)
    build(4)
    tok_recv(3, 1)
    got(wq, ("az", 0, 4), 1)
    build(5)
    own_tok.wait()
    for copy in local:
        copy.wait()
    recv("sq", wq.at[sib_rows, :])
    recv("sk", wkv.at[sib_rows, 0:HALF])
    recv("sv", wkv.at[sib_rows, HALF:2 * HALF])
    got_lead()
    build(6)
    recv(("ts", 0), tok_all(0, 0))
    for d in (1, 2, 3):
        recv(("ts", d), tok.at[0, 0:2, LEAD:, :])
    project_column(0, 1)
    build(7)
    recv(("t", 4), tok_all(k, far))
    send(("ts", 4), tok_all(k, far), tok_all(k, far), sibling, "ts")
    got(wq, ("az", 1, 4), 2)
    project_column(1, 2)
    got(wq, ("az", 2, 4), 1)
    got(wkv, "bxx", 8)
    project_column(2, 1)
    recv(("ts", 4), tok_all(0, 0))
    project(far, 0)
    project(far, 1)

    streams = (sq, sk, sv)

    def fill(i):
        streams[i][...] = acc[8:, i * HALF:(i + 1) * HALF].astype(BF16).astype(F32)

        @pl.when(chip == 0)
        def _():
            streams[i][0:8, :] = jnp.zeros((8, HALF), F32)

    fill(1)
    fill(2)
    own_taps.wait()
    own_bias.wait()

    def tap(i, j):
        return jnp.where(k == 0, taps_s[i, j:j + 1, 0:HALF], taps_s[i, j:j + 1, HALF:])

    def filtered(i, start, size):
        s = streams[i]
        return (tap(i, 0) * s[8 + start:8 + start + size, :] + tap(i, 1) * s[7 + start:7 + start + size, :]
                + tap(i, 2) * s[6 + start:6 + start + size, :])

    def gate(jj):
        block = filtered(1, jj * 128, 128) * filtered(2, jj * 128, 128)
        gated_s[jj * 128:(jj + 1) * 128, :] = block
        stage[pl.ds(jj, HALF, stride=4), :] = block.T

    for jj in range(4):
        gate(jj)
    snd_g[...] = stage[...].astype(BF16).reshape(CHIPS, 16, HALF)
    exchange(snd_g, rcv_g, 1)
    fill(0)
    for jj in range(4):
        qconv_s[jj * 128:(jj + 1) * 128, :] = filtered(0, jj * 128, 128)
    collect(rcv_g, 1)

    flat[16:, :] = rcv_g[...].astype(F32).reshape(CHIPS * 16, HALF)
    epad[0:16, :] = jnp.zeros((16, HALF), F32)
    ysum[0:16, :] = jnp.zeros((16, HALF), F32)
    low = lax.broadcasted_iota(jnp.int32, (CHIPS, HALF), 1) < BLK
    for c in range(4):
        for jj in range(4):
            now = flat[pl.ds(16 + 4 * c + jj, CHIPS, stride=16), :]
            prev_at = 16 + 4 * c + jj - 1 if jj else 4 * c + 3
            prev = flat[pl.ds(prev_at, CHIPS, stride=16), :]
            epad[pl.ds(16 + 2 * jj + 1, CHIPS, stride=8), :] = now
            epad[pl.ds(16 + 2 * jj, CHIPS, stride=8), :] = pltpu.roll(jnp.where(low, now, prev), BLK, 1)
        for p in range(8):
            windows[:, p * 128:(p + 1) * 128] = epad[2 + 2 * p:2 + 2 * p + 256, :].astype(BF16)
        ysum[16:, :] = jnp.zeros((256, HALF), F32)
        for u in range(4):
            count = 256 - 64 * u
            part = lax.dot_general(
                windows[0:count, :], toep[c, 4 * u:4 * u + 4].reshape(4 * BLK, 1024),
                (((1,), (1,)), ((), ())), preferred_element_type=F32)
            for w in range(2):
                d = 64 * u + 32 * w
                ysum[16 + d:, :] += part[0:256 - d, w * 128:(w + 1) * 128]
        for jj in range(4):
            a = ysum[pl.ds(16 + 2 * jj, CHIPS, stride=8), :]
            b = ysum[pl.ds(2 * jj, CHIPS, stride=8), :]
            e = ysum[pl.ds(16 + 2 * jj + 1, CHIPS, stride=8), :]
            f = ysum[pl.ds(2 * jj + 1, CHIPS, stride=8), :]
            stage[pl.ds(4 * c + jj, CHIPS, stride=16), :] = jnp.where(low, a, f) + pltpu.roll(
                jnp.where(low, e, b), BLK, 1)
    snd_y[...] = stage[...].astype(BF16).reshape(CHIPS, 16, HALF)
    exchange(snd_y, rcv_y, 2)
    collect(rcv_y, 2)

    stage[...] = rcv_y[...].astype(F32).reshape(CHIPS * 16, HALF)
    direct = jnp.where(k == 0, bias_s[:, 0:HALF], bias_s[:, HALF:])

    def mixed(jj):
        conv = stage[pl.ds(jj, HALF, stride=4), :].T
        at_rows = pl.ds(pl.multiple_of(jj * 128, 128), 128)
        return (qconv_s[at_rows, :] * (conv + direct * gated_s[at_rows, :])).astype(BF16)

    for t in (0, 1):
        obuf[t * 128:(t + 1) * 128, :] = mixed(2 * (1 - k) + t)
    send("o", obuf, out.at[:, mine], sibling, "o")
    for t in (0, 1):
        out[t * 128:(t + 1) * 128, mine] = mixed(2 * k + t)
    sent("sq", w_q.at[:, theirs])
    sent("sk", w_k.at[:, theirs])
    sent("sv", w_v.at[:, theirs])
    sent("f", filt.at[:, theirs])
    sent("t", tok.at[0, 0:7, LEAD:, :])
    sent("ts", tok.at[0, :, LEAD:, :])
    sent("wq", wq.at[0:31 * 128, :])
    sent("wkv", wkv.at[0:31 * 128, :])

    @pl.when(k == 1)
    def _():
        sent("lead", tokens.at[ROWS - LEAD:, :])

    sent("leads", tok.at[0, 0:7, 0:LEAD, quarter])
    sent("leadx", tok.at[0, :, 0:LEAD, quarter])
    for n, snd in enumerate((snd_h, snd_g, snd_y)):
        flushed(snd, n)
    sent("o", obuf)
    recv("o", out.at[:, theirs])


def on_device(tokens, w_query, w_key, w_value, short_taps, long_filter, filter_bias):
    hbm = pl.BlockSpec(memory_space=pltpu.HBM)
    dma = pltpu.SemaphoreType.DMA
    return pl.pallas_call(
        kernel,
        out_shape=jax.ShapeDtypeStruct((ROWS, 2 * HALF), BF16),
        in_specs=[hbm] * 7,
        out_specs=pl.BlockSpec(memory_space=pltpu.VMEM),
        scratch_shapes=[
            pltpu.VMEM((2, Y, LEAD + ROWS, KB), BF16),
            pltpu.VMEM((Y * KB, HALF), BF16),
            pltpu.VMEM((Y * KB, 2 * HALF), BF16),
            pltpu.VMEM((LEAD + POS, 3 * HALF), F32),
            pltpu.VMEM((POS + 8, HALF), F32),
            pltpu.VMEM((POS + 8, HALF), F32),
            pltpu.VMEM((POS + 8, HALF), F32),
            pltpu.VMEM((POS, HALF), F32),
            pltpu.VMEM((POS, HALF), F32),
            pltpu.VMEM((POS, HALF), F32),
            pltpu.VMEM((POS, HALF), F32),
            pltpu.VMEM((CHIPS, 16, HALF), BF16),
            pltpu.VMEM((CHIPS, 16, HALF), BF16),
            pltpu.VMEM((CHIPS, 16, HALF), BF16),
            pltpu.VMEM((CHIPS, 16, HALF), BF16),
            pltpu.VMEM((CHIPS, 16, HALF), BF16),
            pltpu.VMEM((CHIPS, 16, HALF), BF16),
            pltpu.VMEM((16 + POS, HALF), F32),
            pltpu.VMEM((16 + 256, HALF), F32),
            pltpu.VMEM((256, 1024), BF16),
            pltpu.VMEM((4, 16, BLK, 1024), BF16),
            pltpu.VMEM((16 + 256, HALF), F32),
            pltpu.VMEM((ROWS, HALF), BF16),
            pltpu.VMEM((3, 3, 2 * HALF), F32),
            pltpu.VMEM((1, 2 * HALF), F32),
            dma((7,)),
            dma((N_SEND,)),
            dma((N_RECV,)),
            dma((3,)),
            dma((3,)),
        ],
        compiler_params=pltpu.CompilerParams(
            collective_id=0, has_side_effects=True, vmem_limit_bytes=61850 * 1024),
        name="hyena",
    )(tokens, w_query, w_key, w_value, short_taps, long_filter, filter_bias.reshape(1, -1))


def solution(mesh):
    return jax.shard_map(
        on_device,
        mesh=mesh,
        in_specs=(
            P(("fsdp", "ctx"), "ch"),
            P(("fsdp", "ctx"), "ch"),
            P(("fsdp", "ctx"), "ch"),
            P(("fsdp", "ctx"), "ch"),
            P(None, None, "ch"),
            P(("fsdp", "ctx"), "ch"),
            P("ch"),
        ),
        out_specs=P(("fsdp", "ctx"), "ch"),
        check_vma=False,
    )
```

```python
import jax
import jax.numpy as jnp
from jax import lax
from jax.experimental import pallas as pl
from jax.experimental.pallas import tpu as pltpu
from jax.sharding import PartitionSpec as P

MESH = pl.DeviceIdType.MESH
X, Z, Y = 4, 8, 8
CHIPS = X * Z
ROWS = 256
HALF = 128
LEAD = 16
POS = 2 * ROWS
KB = 512
BLK = 64
F32 = jnp.float32
BF16 = jnp.bfloat16
N_RECV = 48
N_SEND = 12


def kernel(
    tokens, w_q, w_k, w_v, taps_hbm, filt, bias_hbm, out,
    tok, wq, wkv, acc, sq, sk, sv, gated_s, qconv_s, filt_s,
    stage, snd_h, rcv_h, snd_g, rcv_g, snd_y, rcv_y, flat, epad, windows, toep, ysum, obuf,
    taps_s, bias_s, loc_sem, ss, rs, ss_x, rs_x,
):
    x = lax.axis_index("fsdp")
    cx = lax.axis_index("ctx")
    y = lax.axis_index("ch")
    z = lax.div(cx, 2)
    k = lax.rem(cx, 2)
    chip = x * Z + z

    def at(xx, zz, kk, yy):
        return (xx, zz * 2 + kk, yy)

    def xm(d):
        return lax.rem(x + d + X, X)

    def zm(d):
        return lax.rem(z + d + Z, Z)

    def ym(d):
        return lax.rem(y + d + Y, Y)

    sibling = at(x, z, 1 - k, y)
    x_to = {s: at(xm(s), z, k, y) for s in (1, -1, 2)}
    z_to = {s: at(x, zm(s), k, y) for s in (1, -1, 2, -2)}
    y_to = {s: at(x, z, k, ym(s)) for s in (1, -1)}

    def peer(r):
        p = lax.rem(chip + r, CHIPS)
        return p, at(lax.div(p, Z), lax.rem(p, Z), k, y)

    barrier = pltpu.get_barrier_semaphore()
    x_across = {s: at(xm(s), z, 1 - k, y) for s in (1, -1, 2)}
    z_across = {s: at(x, zm(s), 1 - k, y) for s in (1, -1, 2, -2)}
    previous = lax.rem(chip + CHIPS - 1, CHIPS)
    greeted = [sibling, at(lax.div(previous, Z), lax.rem(previous, Z), 1 - k, y)]
    greeted += [at(x, z, k, ym(d)) for d in range(1, Y)]
    greeted += list(x_across.values()) + list(z_across.values())
    for target in greeted:
        pl.semaphore_signal(barrier, inc=1, device_id=target, device_id_type=MESH)

    def greet(r, carry):
        _, target = peer(r)
        pl.semaphore_signal(barrier, inc=1, device_id=target, device_id_type=MESH)
        return carry

    lax.fori_loop(1, CHIPS, greet, 0)
    pl.semaphore_wait(barrier, CHIPS - 1 + len(greeted))

    arrivals, departures = {}, {}

    def send(name, src, dst, target, group):
        n = arrivals.setdefault(name, len(arrivals))
        g = departures.setdefault(group, len(departures))
        pltpu.make_async_remote_copy(
            src_ref=src, dst_ref=dst, send_sem=ss.at[g], recv_sem=rs.at[n],
            device_id=target, device_id_type=MESH).start()

    def recv(name, ref):
        pltpu.make_async_copy(ref, ref, rs.at[arrivals[name]]).wait()

    def sent(group, ref):
        pltpu.make_async_copy(ref, ref, ss.at[departures[group]]).wait()

    mine = pl.ds(pl.multiple_of(k * HALF, HALF), HALF)
    theirs = pl.ds(pl.multiple_of((1 - k) * HALF, HALF), HALF)

    own_rows = pl.ds(pl.multiple_of(chip * 128 + k * 64, 64), 64)
    sib_rows = pl.ds(pl.multiple_of(chip * 128 + (1 - k) * 64, 64), 64)
    my_lags = pl.ds(pl.multiple_of(k * ROWS, ROWS), ROWS)
    sib_lags = pl.ds(pl.multiple_of((1 - k) * ROWS, ROWS), ROWS)

    def tok_half(block, h):
        return tok.at[k, block, LEAD + h * 128:LEAD + (h + 1) * 128, :]

    def tok_all(half, block):
        return tok.at[half, block, LEAD:, :]

    quarter = pl.ds(pl.multiple_of(k * 256, 256), 256)
    nxt = lax.rem(chip + 1, CHIPS)

    def send_lead():
        @pl.when(k == 1)
        def _():
            for kk in (0, 1):
                cut = pl.ds(kk * 256, 256)
                send("lead", tokens.at[ROWS - LEAD:, cut], tok.at[0, y, 0:LEAD, cut],
                     at(lax.div(nxt, Z), lax.rem(nxt, Z), kk, y), "lead")

    def spread_lead():
        ref = tok.at[0, y, 0:LEAD, quarter]
        recv("lead", ref)
        for d in range(1, Y):
            send("leads", ref, ref, at(x, z, k, ym(d)), "leads")

    def share_lead():
        recv("leads", tok.at[0, 0:7, 0:LEAD, quarter])
        ref = tok.at[0, :, 0:LEAD, quarter]
        send("leadx", ref, ref, sibling, "leadx")

    def got_lead():
        recv("leadx", tok.at[0, :, 0:LEAD, quarter])

    both = (1, -1)
    side = {1: 0, -1: 1}

    def tok_recv(d, h):
        recv(("t", d, h), tok_all(0, 0))
        for s in (1, -1):
            block = ym(-s * d)
            half_block = tok_half(block, h)
            if d < 3:
                send(("t", d + 1, h), half_block, half_block, y_to[s], "t")
            elif h == side[s]:
                send(("t", 4), half_block, half_block, y_to[s], "t")
            if h == 1:
                send(("ts", d), tok_all(k, block), tok_all(k, block), sibling, "ts")

    def wrows(xx, zz, half=None):
        base = (xx * Z + zz) * 128
        if half is None:
            return pl.ds(pl.multiple_of(base, 128), 128)
        return pl.ds(pl.multiple_of(base + 64 * half, 64), 64)

    def hop(buf, name, xx, zz, target, half=None):
        ref = buf.at[wrows(xx, zz, half), :]
        send(name, ref, ref, target, "wq" if buf is wq else "wkv")

    def got(buf, name, blocks=2):
        recv(name, buf.at[0:128 * blocks, :])


    def first_hop(buf, name, steps, near, across):
        for s in steps:
            for columns, target in ((mine, near[s]), (theirs, across[s])):
                if buf is wq:
                    send(name, w_q.at[:, columns], wq.at[own_rows, :], target, "wq")
                else:
                    send(name, w_k.at[:, columns], wkv.at[own_rows, 0:HALF], target, "wkv")
                    send(name, w_v.at[:, columns], wkv.at[own_rows, HALF:2 * HALF], target, "wkv")

    def pass_ax():
        got(wq, "ax")
        for s in both:
            for b in both:
                hop(wq, ("az", 1, 1), xm(b), z, z_to[s])

    def pass_axx():
        got(wq, "axx", 1)
        for s in both:
            hop(wq, ("az", 2, 1), xm(2), z, z_to[s])

    def pass_az(b, d):
        columns = both if b == 1 else (b,)
        got(wq, ("az", b, d), 2 * len(columns))
        for col in columns:
            for s in both:
                hop(wq, ("az", b, d + 1), xm(col), zm(-s * d), z_to[s], side[s] if d == 3 else None)

    def pass_bz(d):
        got(wkv, ("bz", d))
        if d > 1:
            for s in both:
                hop(wkv, ("bz", d + 1), x, zm(-s * d), z_to[s], side[s] if d == 3 else None)
        for s in both:
            for m in (d, -d):
                hop(wkv, ("bx", d), x, zm(m), x_to[s])

    def pass_bz4():
        got(wkv, ("bz", 4), 1)
        for s in both:
            hop(wkv, ("bx", 4), x, zm(4), x_to[s])

    def pass_bx(d):
        rows = (0,) if d == 0 else (4,) if d == 4 else (d, -d)
        got(wkv, ("bx", d), 2 * len(rows))
        for m in rows:
            for s in both:
                hop(wkv, "bxx", xm(-s), zm(m), x_to[s], side[s])

    send_lead()
    for h in (0, 1):
        for s in (1, -1):
            send(("t", 1, h), tokens.at[h * 128:(h + 1) * 128, :], tok_half(y, h), y_to[s], "t")
    first_hop(wkv, ("bz", 1), both, z_to, z_across)
    first_hop(wq, "ax", both, x_to, x_across)
    first_hop(wkv, ("bz", 2), (2, -2), z_to, z_across)
    first_hop(wq, "axx", (2,), x_to, x_across)
    first_hop(wkv, ("bx", 0), both, x_to, x_across)
    first_hop(wq, ("az", 0, 1), both, z_to, z_across)
    send("sq", w_q.at[:, theirs], wq.at[own_rows, :], sibling, "sq")
    send("sk", w_k.at[:, theirs], wkv.at[own_rows, 0:HALF], sibling, "sk")
    send("sv", w_v.at[:, theirs], wkv.at[own_rows, HALF:2 * HALF], sibling, "sv")
    local = [
        pltpu.make_async_copy(w_q.at[:, mine], wq.at[own_rows, :], loc_sem.at[0]),
        pltpu.make_async_copy(w_k.at[:, mine], wkv.at[own_rows, 0:HALF], loc_sem.at[1]),
        pltpu.make_async_copy(w_v.at[:, mine], wkv.at[own_rows, HALF:2 * HALF], loc_sem.at[2]),
    ]
    for copy in local:
        copy.start()

    own_tok = pltpu.make_async_copy(tokens, tok_all(k, y), loc_sem.at[3])
    own_tok.start()
    send(("ts", 0), tokens, tok_all(k, y), sibling, "ts")
    send("f", filt.at[:, theirs], filt_s.at[my_lags, :], sibling, "f")
    own_filt = pltpu.make_async_copy(filt.at[:, mine], filt_s.at[my_lags, :], loc_sem.at[4])
    own_filt.start()
    own_taps = pltpu.make_async_copy(taps_hbm, taps_s, loc_sem.at[5])
    own_taps.start()
    own_bias = pltpu.make_async_copy(bias_hbm, bias_s, loc_sem.at[6])
    own_bias.start()


    offsets = sorted(
        ((dx, dz) for dx in range(X) for dz in range(Z) if dx or dz),
        key=lambda o: -min(o[0], X - o[0]) - min(o[1], Z - o[1]))

    def exchange(snd, rcv, n):
        for dx, dz in offsets:
            px, pz = xm(dx), zm(dz)
            pltpu.make_async_remote_copy(
                src_ref=snd.at[px * Z + pz], dst_ref=rcv.at[chip], send_sem=ss_x.at[n],
                recv_sem=rs_x.at[n], device_id=at(px, pz, k, y), device_id_type=MESH).start()
        rcv[chip] = snd[chip]

    def collect(rcv, n):
        all_but_one = rcv.at[0:CHIPS - 1]
        pltpu.make_async_copy(all_but_one, all_but_one, rs_x.at[n]).wait()

    def flushed(snd, n):
        all_but_one = snd.at[0:CHIPS - 1]
        pltpu.make_async_copy(all_but_one, all_but_one, ss_x.at[n]).wait()

    def send_filter():
        own_filt.wait()
        recv("f", filt_s.at[sib_lags, :])
        row_i = lax.broadcasted_iota(jnp.int32, (HALF, HALF), 0)
        col_i = lax.broadcasted_iota(jnp.int32, (HALF, HALF), 1)
        flip = (row_i + col_i == HALF - 1).astype(BF16)
        for jj in range(4):
            block = filt_s[jj * 128:(jj + 1) * 128, :].T.astype(BF16)
            stage[pl.ds(jj, HALF, stride=4), :] = jnp.dot(block, flip, preferred_element_type=F32)
        snd_h[...] = stage[...].astype(BF16).reshape(CHIPS, 16, HALF)
        exchange(snd_h, rcv_h, 0)

    def got_filter():
        collect(rcv_h, 0)
        flat[0:16, :] = jnp.zeros((16, HALF), F32)
        flat[16:, :] = rcv_h[...].astype(F32).reshape(CHIPS * 16, HALF)

    lane = lax.broadcasted_iota(jnp.int32, (BLK, HALF), 1)
    sub = lax.broadcasted_iota(jnp.int32, (BLK, HALF), 0)
    keep = lane + (BLK - 1) - sub < HALF

    def shifted_rows(c, v):
        j = 127 - v
        row = 16 + (j // 4) * 16 + 4 * c + j % 4
        wide = jnp.broadcast_to(flat[pl.ds(row, 1), :], (BLK, HALF))
        return pltpu.roll(wide, HALF - BLK + 1, 1, stride=1, stride_axis=0)

    def build(piece):
        c, first = piece // 2, piece % 2 * 8

        def body(d1, later):
            for p in range(7, -1, -1):
                now = shifted_rows(c, (15 - d1) * 8 + p)
                toep[c, d1, :, p * 128:(p + 1) * 128] = jnp.where(keep, now, later).astype(BF16)
                later = now
            return later

        carried = jnp.zeros((BLK, HALF), F32) if first == 0 else shifted_rows(c, (16 - first) * 8)
        lax.fori_loop(first, first + 8, body, carried)

    def project(block, half):
        rows = pl.ds(pl.multiple_of(block * KB, KB), KB)
        if half == 0:
            a, at_rows = tok[0, block], slice(0, LEAD + ROWS)
        else:
            a, at_rows = tok[1, block, LEAD:, :], slice(LEAD + ROWS, LEAD + POS)
        acc[at_rows, 0:HALF] += jnp.dot(a, wq[rows, :], preferred_element_type=F32)
        acc[at_rows, HALF:] += jnp.dot(a, wkv[rows, :], preferred_element_type=F32)

    far = ym(4)

    def project_column(first, count):
        def body(t, carry):
            block = 2 * xm(first + 2 * lax.div(t, 2)) + lax.rem(t, 2)

            @pl.when(block != far)
            def _():
                project(block, 0)
                project(block, 1)

            return carry

        lax.fori_loop(0, 2 * count, body, 0)

    acc[...] = jnp.zeros_like(acc)
    spread_lead()
    pass_ax()
    pass_bz(1)
    tok_recv(1, 0)
    got(wq, "axx", 1)
    for s in both:
        hop(wq, ("az", 2, 1), xm(2), z, z_to[s])
    pass_bz(2)
    pass_bx(0)
    pass_az(0, 1)
    tok_recv(1, 1)
    send_filter()
    pass_az(1, 1)
    pass_bx(1)
    pass_az(2, 1)
    tok_recv(2, 0)
    share_lead()
    pass_bx(2)
    pass_bz(3)
    pass_az(0, 2)
    got_filter()
    build(0)
    tok_recv(2, 1)
    pass_az(1, 2)
    build(1)
    pass_az(2, 2)
    pass_bz4()
    pass_az(0, 3)
    build(2)
    tok_recv(3, 0)
    pass_bx(3)
    pass_az(1, 3)
    build(3)
    pass_bx(4)
    pass_az(2, 3)
    tok_recv(3, 1)
    got(wq, ("az", 0, 4), 1)
    own_tok.wait()
    for copy in local:
        copy.wait()
    recv("sq", wq.at[sib_rows, :])
    recv("sk", wkv.at[sib_rows, 0:HALF])
    recv("sv", wkv.at[sib_rows, HALF:2 * HALF])
    got_lead()
    recv(("ts", 0), tok_all(0, 0))
    for d in (1, 2, 3):
        recv(("ts", d), tok.at[0, 0:2, LEAD:, :])
    project_column(0, 1)
    recv(("t", 4), tok_all(k, far))
    send(("ts", 4), tok_all(k, far), tok_all(k, far), sibling, "ts")
    got(wq, ("az", 1, 4), 2)
    project_column(1, 2)
    got(wq, ("az", 2, 4), 1)
    got(wkv, "bxx", 8)
    project_column(2, 1)
    recv(("ts", 4), tok_all(0, 0))
    project(far, 0)
    project(far, 1)

    streams = (sq, sk, sv)

    def fill(i):
        streams[i][...] = acc[8:, i * HALF:(i + 1) * HALF].astype(BF16).astype(F32)

        @pl.when(chip == 0)
        def _():
            streams[i][0:8, :] = jnp.zeros((8, HALF), F32)

    fill(1)
    fill(2)
    own_taps.wait()
    own_bias.wait()

    def tap(i, j):
        return jnp.where(k == 0, taps_s[i, j:j + 1, 0:HALF], taps_s[i, j:j + 1, HALF:])

    def filtered(i, start, size):
        s = streams[i]
        return (tap(i, 0) * s[8 + start:8 + start + size, :] + tap(i, 1) * s[7 + start:7 + start + size, :]
                + tap(i, 2) * s[6 + start:6 + start + size, :])

    def gate(jj):
        block = filtered(1, jj * 128, 128) * filtered(2, jj * 128, 128)
        gated_s[jj * 128:(jj + 1) * 128, :] = block
        stage[pl.ds(jj, HALF, stride=4), :] = block.T

    for jj in range(4):
        gate(jj)
    snd_g[...] = stage[...].astype(BF16).reshape(CHIPS, 16, HALF)
    exchange(snd_g, rcv_g, 1)
    for piece in (4, 5, 6, 7):
        build(piece)
    fill(0)
    for jj in range(4):
        qconv_s[jj * 128:(jj + 1) * 128, :] = filtered(0, jj * 128, 128)
    collect(rcv_g, 1)

    flat[16:, :] = rcv_g[...].astype(F32).reshape(CHIPS * 16, HALF)
    epad[0:16, :] = jnp.zeros((16, HALF), F32)
    ysum[0:16, :] = jnp.zeros((16, HALF), F32)
    low = lax.broadcasted_iota(jnp.int32, (CHIPS, HALF), 1) < BLK
    for c in range(4):
        for jj in range(4):
            now = flat[pl.ds(16 + 4 * c + jj, CHIPS, stride=16), :]
            prev_at = 16 + 4 * c + jj - 1 if jj else 4 * c + 3
            prev = flat[pl.ds(prev_at, CHIPS, stride=16), :]
            epad[pl.ds(16 + 2 * jj + 1, CHIPS, stride=8), :] = now
            epad[pl.ds(16 + 2 * jj, CHIPS, stride=8), :] = pltpu.roll(jnp.where(low, now, prev), BLK, 1)
        for p in range(8):
            windows[:, p * 128:(p + 1) * 128] = epad[2 + 2 * p:2 + 2 * p + 256, :].astype(BF16)
        ysum[16:, :] = jnp.zeros((256, HALF), F32)
        for u in range(4):
            count = 256 - 64 * u
            part = lax.dot_general(
                windows[0:count, :], toep[c, 4 * u:4 * u + 4].reshape(4 * BLK, 1024),
                (((1,), (1,)), ((), ())), preferred_element_type=F32)
            for w in range(2):
                d = 64 * u + 32 * w
                ysum[16 + d:, :] += part[0:256 - d, w * 128:(w + 1) * 128]
        for jj in range(4):
            a = ysum[pl.ds(16 + 2 * jj, CHIPS, stride=8), :]
            b = ysum[pl.ds(2 * jj, CHIPS, stride=8), :]
            e = ysum[pl.ds(16 + 2 * jj + 1, CHIPS, stride=8), :]
            f = ysum[pl.ds(2 * jj + 1, CHIPS, stride=8), :]
            stage[pl.ds(4 * c + jj, CHIPS, stride=16), :] = jnp.where(low, a, f) + pltpu.roll(
                jnp.where(low, e, b), BLK, 1)
    snd_y[...] = stage[...].astype(BF16).reshape(CHIPS, 16, HALF)
    exchange(snd_y, rcv_y, 2)
    collect(rcv_y, 2)

    stage[...] = rcv_y[...].astype(F32).reshape(CHIPS * 16, HALF)
    direct = jnp.where(k == 0, bias_s[:, 0:HALF], bias_s[:, HALF:])

    def mixed(jj):
        conv = stage[pl.ds(jj, HALF, stride=4), :].T
        at_rows = pl.ds(pl.multiple_of(jj * 128, 128), 128)
        return (qconv_s[at_rows, :] * (conv + direct * gated_s[at_rows, :])).astype(BF16)

    for t in (0, 1):
        obuf[t * 128:(t + 1) * 128, :] = mixed(2 * (1 - k) + t)
    send("o", obuf, out.at[:, mine], sibling, "o")
    for t in (0, 1):
        out[t * 128:(t + 1) * 128, mine] = mixed(2 * k + t)
    sent("sq", w_q.at[:, theirs])
    sent("sk", w_k.at[:, theirs])
    sent("sv", w_v.at[:, theirs])
    sent("f", filt.at[:, theirs])
    sent("t", tok.at[0, 0:7, LEAD:, :])
    sent("ts", tok.at[0, :, LEAD:, :])
    sent("wq", wq.at[0:31 * 128, :])
    sent("wkv", wkv.at[0:31 * 128, :])

    @pl.when(k == 1)
    def _():
        sent("lead", tokens.at[ROWS - LEAD:, :])

    sent("leads", tok.at[0, 0:7, 0:LEAD, quarter])
    sent("leadx", tok.at[0, :, 0:LEAD, quarter])
    for n, snd in enumerate((snd_h, snd_g, snd_y)):
        flushed(snd, n)
    sent("o", obuf)
    recv("o", out.at[:, theirs])


def on_device(tokens, w_query, w_key, w_value, short_taps, long_filter, filter_bias):
    hbm = pl.BlockSpec(memory_space=pltpu.HBM)
    dma = pltpu.SemaphoreType.DMA
    return pl.pallas_call(
        kernel,
        out_shape=jax.ShapeDtypeStruct((ROWS, 2 * HALF), BF16),
        in_specs=[hbm] * 7,
        out_specs=pl.BlockSpec(memory_space=pltpu.VMEM),
        scratch_shapes=[
            pltpu.VMEM((2, Y, LEAD + ROWS, KB), BF16),
            pltpu.VMEM((Y * KB, HALF), BF16),
            pltpu.VMEM((Y * KB, 2 * HALF), BF16),
            pltpu.VMEM((LEAD + POS, 3 * HALF), F32),
            pltpu.VMEM((POS + 8, HALF), F32),
            pltpu.VMEM((POS + 8, HALF), F32),
            pltpu.VMEM((POS + 8, HALF), F32),
            pltpu.VMEM((POS, HALF), F32),
            pltpu.VMEM((POS, HALF), F32),
            pltpu.VMEM((POS, HALF), F32),
            pltpu.VMEM((POS, HALF), F32),
            pltpu.VMEM((CHIPS, 16, HALF), BF16),
            pltpu.VMEM((CHIPS, 16, HALF), BF16),
            pltpu.VMEM((CHIPS, 16, HALF), BF16),
            pltpu.VMEM((CHIPS, 16, HALF), BF16),
            pltpu.VMEM((CHIPS, 16, HALF), BF16),
            pltpu.VMEM((CHIPS, 16, HALF), BF16),
            pltpu.VMEM((16 + POS, HALF), F32),
            pltpu.VMEM((16 + 256, HALF), F32),
            pltpu.VMEM((256, 1024), BF16),
            pltpu.VMEM((4, 16, BLK, 1024), BF16),
            pltpu.VMEM((16 + 256, HALF), F32),
            pltpu.VMEM((ROWS, HALF), BF16),
            pltpu.VMEM((3, 3, 2 * HALF), F32),
            pltpu.VMEM((1, 2 * HALF), F32),
            dma((7,)),
            dma((N_SEND,)),
            dma((N_RECV,)),
            dma((3,)),
            dma((3,)),
        ],
        compiler_params=pltpu.CompilerParams(
            collective_id=0, has_side_effects=True, vmem_limit_bytes=61850 * 1024),
        name="hyena",
    )(tokens, w_query, w_key, w_value, short_taps, long_filter, filter_bias.reshape(1, -1))


def solution(mesh):
    return jax.shard_map(
        on_device,
        mesh=mesh,
        in_specs=(
            P(("fsdp", "ctx"), "ch"),
            P(("fsdp", "ctx"), "ch"),
            P(("fsdp", "ctx"), "ch"),
            P(("fsdp", "ctx"), "ch"),
            P(None, None, "ch"),
            P(("fsdp", "ctx"), "ch"),
            P("ch"),
        ),
        out_specs=P(("fsdp", "ctx"), "ch"),
        check_vma=False,
    )
```

```python
import jax
import jax.numpy as jnp
from jax import lax
from jax.experimental import pallas as pl
from jax.experimental.pallas import tpu as pltpu
from jax.sharding import PartitionSpec as P

MESH = pl.DeviceIdType.MESH
X, Z, Y = 4, 8, 8
CHIPS = X * Z
ROWS = 256
HALF = 128
LEAD = 16
POS = 2 * ROWS
KB = 512
BLK = 64
F32 = jnp.float32
BF16 = jnp.bfloat16
N_RECV = 48
N_SEND = 12


def kernel(
    tokens, w_q, w_k, w_v, taps_hbm, filt, bias_hbm, out,
    tok, wq, wkv, acc, sq, sk, sv, gated_s, qconv_s, filt_s,
    stage, snd_h, rcv_h, snd_g, rcv_g, snd_y, rcv_y, flat, epad, windows, toep, ysum, obuf,
    taps_s, bias_s, loc_sem, ss, rs, ss_x, rs_x,
):
    x = lax.axis_index("fsdp")
    cx = lax.axis_index("ctx")
    y = lax.axis_index("ch")
    z = lax.div(cx, 2)
    k = lax.rem(cx, 2)
    chip = x * Z + z

    def at(xx, zz, kk, yy):
        return (xx, zz * 2 + kk, yy)

    def xm(d):
        return lax.rem(x + d + X, X)

    def zm(d):
        return lax.rem(z + d + Z, Z)

    def ym(d):
        return lax.rem(y + d + Y, Y)

    sibling = at(x, z, 1 - k, y)
    x_to = {s: at(xm(s), z, k, y) for s in (1, -1, 2)}
    z_to = {s: at(x, zm(s), k, y) for s in (1, -1, 2, -2)}
    y_to = {s: at(x, z, k, ym(s)) for s in (1, -1)}

    offsets = sorted(
        ((dx, dz) for dx in range(X) for dz in range(Z) if dx or dz),
        key=lambda o: -min(o[0], X - o[0]) - min(o[1], Z - o[1]))

    barrier = pltpu.get_barrier_semaphore()
    x_across = {s: at(xm(s), z, 1 - k, y) for s in (1, -1, 2)}
    z_across = {s: at(x, zm(s), 1 - k, y) for s in (1, -1, 2, -2)}
    previous = lax.rem(chip + CHIPS - 1, CHIPS)
    greeted = [sibling, at(lax.div(previous, Z), lax.rem(previous, Z), 1 - k, y)]
    greeted += [at(x, z, k, ym(d)) for d in range(1, Y)]
    greeted += list(x_across.values()) + list(z_across.values())
    for target in greeted:
        pl.semaphore_signal(barrier, inc=1, device_id=target, device_id_type=MESH)

    for dx, dz in offsets:
        pl.semaphore_signal(barrier, inc=1, device_id=at(xm(dx), zm(dz), k, y), device_id_type=MESH)
    pl.semaphore_wait(barrier, CHIPS - 1 + len(greeted))

    arrivals, departures = {}, {}

    def send(name, src, dst, target, group):
        n = arrivals.setdefault(name, len(arrivals))
        g = departures.setdefault(group, len(departures))
        pltpu.make_async_remote_copy(
            src_ref=src, dst_ref=dst, send_sem=ss.at[g], recv_sem=rs.at[n],
            device_id=target, device_id_type=MESH).start()

    def recv(name, ref):
        pltpu.make_async_copy(ref, ref, rs.at[arrivals[name]]).wait()

    def sent(group, ref):
        pltpu.make_async_copy(ref, ref, ss.at[departures[group]]).wait()

    mine = pl.ds(pl.multiple_of(k * HALF, HALF), HALF)
    theirs = pl.ds(pl.multiple_of((1 - k) * HALF, HALF), HALF)

    own_rows = pl.ds(pl.multiple_of(chip * 128 + k * 64, 64), 64)
    sib_rows = pl.ds(pl.multiple_of(chip * 128 + (1 - k) * 64, 64), 64)
    my_lags = pl.ds(pl.multiple_of(k * ROWS, ROWS), ROWS)
    sib_lags = pl.ds(pl.multiple_of((1 - k) * ROWS, ROWS), ROWS)

    def tok_half(block, h):
        return tok.at[k, block, LEAD + h * 128:LEAD + (h + 1) * 128, :]

    def tok_all(half, block):
        return tok.at[half, block, LEAD:, :]

    quarter = pl.ds(pl.multiple_of(k * 256, 256), 256)
    nxt = lax.rem(chip + 1, CHIPS)

    def send_lead():
        @pl.when(k == 1)
        def _():
            for kk in (0, 1):
                cut = pl.ds(kk * 256, 256)
                send("lead", tokens.at[ROWS - LEAD:, cut], tok.at[0, y, 0:LEAD, cut],
                     at(lax.div(nxt, Z), lax.rem(nxt, Z), kk, y), "lead")

    def spread_lead():
        ref = tok.at[0, y, 0:LEAD, quarter]
        recv("lead", ref)
        for d in range(1, Y):
            send("leads", ref, ref, at(x, z, k, ym(d)), "leads")

    def share_lead():
        recv("leads", tok.at[0, 0:7, 0:LEAD, quarter])
        ref = tok.at[0, :, 0:LEAD, quarter]
        send("leadx", ref, ref, sibling, "leadx")

    def got_lead():
        recv("leadx", tok.at[0, :, 0:LEAD, quarter])

    both = (1, -1)
    side = {1: 0, -1: 1}

    def tok_recv(d, h):
        recv(("t", d, h), tok_all(0, 0))
        for s in (1, -1):
            block = ym(-s * d)
            half_block = tok_half(block, h)
            if d < 3:
                send(("t", d + 1, h), half_block, half_block, y_to[s], "t")
            elif h == side[s]:
                send(("t", 4), half_block, half_block, y_to[s], "t")
            if h == 1:
                send(("ts", d), tok_all(k, block), tok_all(k, block), sibling, "ts")

    def wrows(xx, zz, half=None):
        base = (xx * Z + zz) * 128
        if half is None:
            return pl.ds(pl.multiple_of(base, 128), 128)
        return pl.ds(pl.multiple_of(base + 64 * half, 64), 64)

    def hop(buf, name, xx, zz, target, half=None):
        ref = buf.at[wrows(xx, zz, half), :]
        send(name, ref, ref, target, "wq" if buf is wq else "wkv")

    def got(buf, name, blocks=2):
        recv(name, buf.at[0:128 * blocks, :])


    def first_hop(buf, name, steps, near, across):
        for s in steps:
            for columns, target in ((mine, near[s]), (theirs, across[s])):
                if buf is wq:
                    send(name, w_q.at[:, columns], wq.at[own_rows, :], target, "wq")
                else:
                    send(name, w_k.at[:, columns], wkv.at[own_rows, 0:HALF], target, "wkv")
                    send(name, w_v.at[:, columns], wkv.at[own_rows, HALF:2 * HALF], target, "wkv")

    def pass_ax():
        got(wq, "ax")
        for s in both:
            for b in both:
                hop(wq, ("az", 1, 1), xm(b), z, z_to[s])

    def pass_axx():
        got(wq, "axx", 1)
        for s in both:
            hop(wq, ("az", 2, 1), xm(2), z, z_to[s])

    def pass_az(b, d):
        columns = both if b == 1 else (b,)
        got(wq, ("az", b, d), 2 * len(columns))
        for col in columns:
            for s in both:
                hop(wq, ("az", b, d + 1), xm(col), zm(-s * d), z_to[s], side[s] if d == 3 else None)

    def pass_bz(d):
        got(wkv, ("bz", d))
        if d > 1:
            for s in both:
                hop(wkv, ("bz", d + 1), x, zm(-s * d), z_to[s], side[s] if d == 3 else None)
        for s in both:
            for m in (d, -d):
                hop(wkv, ("bx", d), x, zm(m), x_to[s])

    def pass_bz4():
        got(wkv, ("bz", 4), 1)
        for s in both:
            hop(wkv, ("bx", 4), x, zm(4), x_to[s])

    def pass_bx(d):
        rows = (0,) if d == 0 else (4,) if d == 4 else (d, -d)
        got(wkv, ("bx", d), 2 * len(rows))
        for m in rows:
            for s in both:
                hop(wkv, "bxx", xm(-s), zm(m), x_to[s], side[s])

    send_lead()
    for h in (0, 1):
        for s in (1, -1):
            send(("t", 1, h), tokens.at[h * 128:(h + 1) * 128, :], tok_half(y, h), y_to[s], "t")
    first_hop(wkv, ("bz", 1), both, z_to, z_across)
    first_hop(wq, "ax", both, x_to, x_across)
    first_hop(wkv, ("bz", 2), (2, -2), z_to, z_across)
    first_hop(wq, "axx", (2,), x_to, x_across)
    first_hop(wkv, ("bx", 0), both, x_to, x_across)
    first_hop(wq, ("az", 0, 1), both, z_to, z_across)
    send("sq", w_q.at[:, theirs], wq.at[own_rows, :], sibling, "sq")
    send("sk", w_k.at[:, theirs], wkv.at[own_rows, 0:HALF], sibling, "sk")
    send("sv", w_v.at[:, theirs], wkv.at[own_rows, HALF:2 * HALF], sibling, "sv")
    local = [
        pltpu.make_async_copy(w_q.at[:, mine], wq.at[own_rows, :], loc_sem.at[0]),
        pltpu.make_async_copy(w_k.at[:, mine], wkv.at[own_rows, 0:HALF], loc_sem.at[1]),
        pltpu.make_async_copy(w_v.at[:, mine], wkv.at[own_rows, HALF:2 * HALF], loc_sem.at[2]),
    ]
    for copy in local:
        copy.start()

    own_tok = pltpu.make_async_copy(tokens, tok_all(k, y), loc_sem.at[3])
    own_tok.start()
    send(("ts", 0), tokens, tok_all(k, y), sibling, "ts")
    send("f", filt.at[:, theirs], filt_s.at[my_lags, :], sibling, "f")
    own_filt = pltpu.make_async_copy(filt.at[:, mine], filt_s.at[my_lags, :], loc_sem.at[4])
    own_filt.start()
    own_taps = pltpu.make_async_copy(taps_hbm, taps_s, loc_sem.at[5])
    own_taps.start()
    own_bias = pltpu.make_async_copy(bias_hbm, bias_s, loc_sem.at[6])
    own_bias.start()


    def exchange(snd, rcv, n):
        for dx, dz in offsets:
            px, pz = xm(dx), zm(dz)
            pltpu.make_async_remote_copy(
                src_ref=snd.at[px * Z + pz], dst_ref=rcv.at[chip], send_sem=ss_x.at[n],
                recv_sem=rs_x.at[n], device_id=at(px, pz, k, y), device_id_type=MESH).start()
        rcv[chip] = snd[chip]

    def collect(rcv, n):
        all_but_one = rcv.at[0:CHIPS - 1]
        pltpu.make_async_copy(all_but_one, all_but_one, rs_x.at[n]).wait()

    def flushed(snd, n):
        all_but_one = snd.at[0:CHIPS - 1]
        pltpu.make_async_copy(all_but_one, all_but_one, ss_x.at[n]).wait()

    def send_filter():
        own_filt.wait()
        recv("f", filt_s.at[sib_lags, :])
        row_i = lax.broadcasted_iota(jnp.int32, (HALF, HALF), 0)
        col_i = lax.broadcasted_iota(jnp.int32, (HALF, HALF), 1)
        flip = (row_i + col_i == HALF - 1).astype(BF16)
        for jj in range(4):
            block = filt_s[jj * 128:(jj + 1) * 128, :].T.astype(BF16)
            stage[pl.ds(jj, HALF, stride=4), :] = jnp.dot(block, flip, preferred_element_type=F32)
        snd_h[...] = stage[...].astype(BF16).reshape(CHIPS, 16, HALF)
        exchange(snd_h, rcv_h, 0)

    def got_filter():
        collect(rcv_h, 0)
        flat[0:16, :] = jnp.zeros((16, HALF), F32)
        flat[16:, :] = rcv_h[...].astype(F32).reshape(CHIPS * 16, HALF)

    lane = lax.broadcasted_iota(jnp.int32, (BLK, HALF), 1)
    sub = lax.broadcasted_iota(jnp.int32, (BLK, HALF), 0)
    keep = lane + (BLK - 1) - sub < HALF

    def shifted_rows(c, v):
        j = 127 - v
        row = 16 + (j // 4) * 16 + 4 * c + j % 4
        wide = jnp.broadcast_to(flat[pl.ds(row, 1), :], (BLK, HALF))
        return pltpu.roll(wide, HALF - BLK + 1, 1, stride=1, stride_axis=0)

    def build(piece):
        c, first = piece // 2, piece % 2 * 8

        def body(d1, later):
            for p in range(7, -1, -1):
                now = shifted_rows(c, (15 - d1) * 8 + p)
                toep[c, d1, :, p * 128:(p + 1) * 128] = jnp.where(keep, now, later).astype(BF16)
                later = now
            return later

        carried = jnp.zeros((BLK, HALF), F32) if first == 0 else shifted_rows(c, (16 - first) * 8)
        lax.fori_loop(first, first + 8, body, carried)

    def project(block, half):
        rows = pl.ds(pl.multiple_of(block * KB, KB), KB)
        if half == 0:
            a, at_rows = tok[0, block], slice(0, LEAD + ROWS)
        else:
            a, at_rows = tok[1, block, LEAD:, :], slice(LEAD + ROWS, LEAD + POS)
        acc[at_rows, 0:HALF] += jnp.dot(a, wq[rows, :], preferred_element_type=F32)
        acc[at_rows, HALF:] += jnp.dot(a, wkv[rows, :], preferred_element_type=F32)

    far = ym(4)

    def project_column(first, count):
        def body(t, carry):
            block = 2 * xm(first + 2 * lax.div(t, 2)) + lax.rem(t, 2)

            @pl.when(block != far)
            def _():
                project(block, 0)
                project(block, 1)

            return carry

        lax.fori_loop(0, 2 * count, body, 0)

    acc[...] = jnp.zeros_like(acc)
    send_filter()
    spread_lead()
    pass_ax()
    pass_bz(1)
    tok_recv(1, 0)
    got(wq, "axx", 1)
    for s in both:
        hop(wq, ("az", 2, 1), xm(2), z, z_to[s])
    pass_bz(2)
    pass_bx(0)
    pass_az(0, 1)
    tok_recv(1, 1)
    pass_az(1, 1)
    pass_bx(1)
    pass_az(2, 1)
    tok_recv(2, 0)
    share_lead()
    pass_bx(2)
    pass_bz(3)
    pass_az(0, 2)
    got_filter()
    build(0)
    tok_recv(2, 1)
    pass_az(1, 2)
    build(1)
    pass_az(2, 2)
    pass_bz4()
    pass_az(0, 3)
    build(2)
    tok_recv(3, 0)
    pass_bx(3)
    pass_az(1, 3)
    build(3)
    pass_bx(4)
    pass_az(2, 3)
    tok_recv(3, 1)
    got(wq, ("az", 0, 4), 1)
    own_tok.wait()
    for copy in local:
        copy.wait()
    recv("sq", wq.at[sib_rows, :])
    recv("sk", wkv.at[sib_rows, 0:HALF])
    recv("sv", wkv.at[sib_rows, HALF:2 * HALF])
    got_lead()
    recv(("ts", 0), tok_all(0, 0))
    for d in (1, 2, 3):
        recv(("ts", d), tok.at[0, 0:2, LEAD:, :])
    project_column(0, 1)
    recv(("t", 4), tok_all(k, far))
    send(("ts", 4), tok_all(k, far), tok_all(k, far), sibling, "ts")
    got(wq, ("az", 1, 4), 2)
    project_column(1, 2)
    got(wq, ("az", 2, 4), 1)
    got(wkv, "bxx", 8)
    project_column(2, 1)
    recv(("ts", 4), tok_all(0, 0))
    project(far, 0)
    project(far, 1)

    streams = (sq, sk, sv)

    def fill(i):
        streams[i][...] = acc[8:, i * HALF:(i + 1) * HALF].astype(BF16).astype(F32)

        @pl.when(chip == 0)
        def _():
            streams[i][0:8, :] = jnp.zeros((8, HALF), F32)

    fill(1)
    fill(2)
    own_taps.wait()
    own_bias.wait()

    def tap(i, j):
        return jnp.where(k == 0, taps_s[i, j:j + 1, 0:HALF], taps_s[i, j:j + 1, HALF:])

    def filtered(i, start, size):
        s = streams[i]
        return (tap(i, 0) * s[8 + start:8 + start + size, :] + tap(i, 1) * s[7 + start:7 + start + size, :]
                + tap(i, 2) * s[6 + start:6 + start + size, :])

    def gate(jj):
        block = filtered(1, jj * 128, 128) * filtered(2, jj * 128, 128)
        gated_s[jj * 128:(jj + 1) * 128, :] = block
        stage[pl.ds(jj, HALF, stride=4), :] = block.T

    for jj in range(4):
        gate(jj)
    snd_g[...] = stage[...].astype(BF16).reshape(CHIPS, 16, HALF)
    exchange(snd_g, rcv_g, 1)
    for piece in (4, 5, 6, 7):
        build(piece)
    fill(0)
    for jj in range(4):
        qconv_s[jj * 128:(jj + 1) * 128, :] = filtered(0, jj * 128, 128)
    collect(rcv_g, 1)

    flat[16:, :] = rcv_g[...].astype(F32).reshape(CHIPS * 16, HALF)
    epad[:, 0:16, :] = jnp.zeros((4, 16, HALF), F32)
    ysum[:, 0:16, :] = jnp.zeros((4, 16, HALF), F32)
    ysum[:, 16:, :] = jnp.zeros((4, 256, HALF), F32)
    low = lax.broadcasted_iota(jnp.int32, (CHIPS, HALF), 1) < BLK
    for c in range(4):
        for jj in range(4):
            now = flat[pl.ds(16 + 4 * c + jj, CHIPS, stride=16), :]
            prev_at = 16 + 4 * c + jj - 1 if jj else 4 * c + 3
            prev = flat[pl.ds(prev_at, CHIPS, stride=16), :]
            epad[c, pl.ds(16 + 2 * jj + 1, CHIPS, stride=8), :] = now
            epad[c, pl.ds(16 + 2 * jj, CHIPS, stride=8), :] = pltpu.roll(jnp.where(low, now, prev), BLK, 1)
        for p in range(8):
            windows[c, :, p * 128:(p + 1) * 128] = epad[c, 2 + 2 * p:2 + 2 * p + 256, :].astype(BF16)
        for u in range(4):
            count = 256 - 64 * u
            part = lax.dot_general(
                windows[c, 0:count, :], toep[c, 4 * u:4 * u + 4].reshape(4 * BLK, 1024),
                (((1,), (1,)), ((), ())), preferred_element_type=F32)
            for w in range(2):
                d = 64 * u + 32 * w
                ysum[c, 16 + d:, :] += part[0:256 - d, w * 128:(w + 1) * 128]
        for jj in range(4):
            a = ysum[c, pl.ds(16 + 2 * jj, CHIPS, stride=8), :]
            b = ysum[c, pl.ds(2 * jj, CHIPS, stride=8), :]
            e = ysum[c, pl.ds(16 + 2 * jj + 1, CHIPS, stride=8), :]
            f = ysum[c, pl.ds(2 * jj + 1, CHIPS, stride=8), :]
            stage[pl.ds(4 * c + jj, CHIPS, stride=16), :] = jnp.where(low, a, f) + pltpu.roll(
                jnp.where(low, e, b), BLK, 1)
    snd_y[...] = stage[...].astype(BF16).reshape(CHIPS, 16, HALF)
    exchange(snd_y, rcv_y, 2)
    collect(rcv_y, 2)

    stage[...] = rcv_y[...].astype(F32).reshape(CHIPS * 16, HALF)
    direct = jnp.where(k == 0, bias_s[:, 0:HALF], bias_s[:, HALF:])

    def mixed(jj):
        conv = stage[pl.ds(jj, HALF, stride=4), :].T
        at_rows = pl.ds(pl.multiple_of(jj * 128, 128), 128)
        return (qconv_s[at_rows, :] * (conv + direct * gated_s[at_rows, :])).astype(BF16)

    for t in (0, 1):
        obuf[t * 128:(t + 1) * 128, :] = mixed(2 * (1 - k) + t)
    send("o", obuf, out.at[:, mine], sibling, "o")
    for t in (0, 1):
        out[t * 128:(t + 1) * 128, mine] = mixed(2 * k + t)
    sent("sq", w_q.at[:, theirs])
    sent("sk", w_k.at[:, theirs])
    sent("sv", w_v.at[:, theirs])
    sent("f", filt.at[:, theirs])
    sent("t", tok.at[0, 0:7, LEAD:, :])
    sent("ts", tok.at[0, :, LEAD:, :])
    sent("wq", wq.at[0:31 * 128, :])
    sent("wkv", wkv.at[0:31 * 128, :])

    @pl.when(k == 1)
    def _():
        sent("lead", tokens.at[ROWS - LEAD:, :])

    sent("leads", tok.at[0, 0:7, 0:LEAD, quarter])
    sent("leadx", tok.at[0, :, 0:LEAD, quarter])
    for n, snd in enumerate((snd_h, snd_g, snd_y)):
        flushed(snd, n)
    sent("o", obuf)
    recv("o", out.at[:, theirs])


def on_device(tokens, w_query, w_key, w_value, short_taps, long_filter, filter_bias):
    hbm = pl.BlockSpec(memory_space=pltpu.HBM)
    dma = pltpu.SemaphoreType.DMA
    return pl.pallas_call(
        kernel,
        out_shape=jax.ShapeDtypeStruct((ROWS, 2 * HALF), BF16),
        in_specs=[hbm] * 7,
        out_specs=pl.BlockSpec(memory_space=pltpu.VMEM),
        scratch_shapes=[
            pltpu.VMEM((2, Y, LEAD + ROWS, KB), BF16),
            pltpu.VMEM((Y * KB, HALF), BF16),
            pltpu.VMEM((Y * KB, 2 * HALF), BF16),
            pltpu.VMEM((LEAD + POS, 3 * HALF), F32),
            pltpu.VMEM((POS + 8, HALF), F32),
            pltpu.VMEM((POS + 8, HALF), F32),
            pltpu.VMEM((POS + 8, HALF), F32),
            pltpu.VMEM((POS, HALF), F32),
            pltpu.VMEM((POS, HALF), F32),
            pltpu.VMEM((POS, HALF), F32),
            pltpu.VMEM((POS, HALF), F32),
            pltpu.VMEM((CHIPS, 16, HALF), BF16),
            pltpu.VMEM((CHIPS, 16, HALF), BF16),
            pltpu.VMEM((CHIPS, 16, HALF), BF16),
            pltpu.VMEM((CHIPS, 16, HALF), BF16),
            pltpu.VMEM((CHIPS, 16, HALF), BF16),
            pltpu.VMEM((CHIPS, 16, HALF), BF16),
            pltpu.VMEM((16 + POS, HALF), F32),
            pltpu.VMEM((4, 16 + 256, HALF), F32),
            pltpu.VMEM((4, 256, 1024), BF16),
            pltpu.VMEM((4, 16, BLK, 1024), BF16),
            pltpu.VMEM((4, 16 + 256, HALF), F32),
            pltpu.VMEM((ROWS, HALF), BF16),
            pltpu.VMEM((3, 3, 2 * HALF), F32),
            pltpu.VMEM((1, 2 * HALF), F32),
            dma((7,)),
            dma((N_SEND,)),
            dma((N_RECV,)),
            dma((3,)),
            dma((3,)),
        ],
        compiler_params=pltpu.CompilerParams(
            collective_id=0, has_side_effects=True, vmem_limit_bytes=61850 * 1024),
        name="hyena",
    )(tokens, w_query, w_key, w_value, short_taps, long_filter, filter_bias.reshape(1, -1))


def solution(mesh):
    return jax.shard_map(
        on_device,
        mesh=mesh,
        in_specs=(
            P(("fsdp", "ctx"), "ch"),
            P(("fsdp", "ctx"), "ch"),
            P(("fsdp", "ctx"), "ch"),
            P(("fsdp", "ctx"), "ch"),
            P(None, None, "ch"),
            P(("fsdp", "ctx"), "ch"),
            P("ch"),
        ),
        out_specs=P(("fsdp", "ctx"), "ch"),
        check_vma=False,
    )
```

```python
import jax
import jax.numpy as jnp
from jax import lax
from jax.experimental import pallas as pl
from jax.experimental.pallas import tpu as pltpu
from jax.sharding import PartitionSpec as P

MESH = pl.DeviceIdType.MESH
X, Z, Y = 4, 8, 8
CHIPS = X * Z
ROWS = 256
HALF = 128
LEAD = 16
POS = 2 * ROWS
KB = 512
BLK = 64
F32 = jnp.float32
BF16 = jnp.bfloat16
N_RECV = 48
N_SEND = 12


def kernel(
    tokens, w_q, w_k, w_v, taps_hbm, filt, bias_hbm, out,
    tok, wq, wkv, acc, sq, sk, sv, gated_s, qconv_s, filt_s,
    stage, snd_h, rcv_h, snd_g, rcv_g, snd_y, rcv_y, flat, epad, windows, toep, ysum, obuf,
    taps_s, bias_s, loc_sem, ss, rs, ss_x, rs_x,
):
    x = lax.axis_index("fsdp")
    cx = lax.axis_index("ctx")
    y = lax.axis_index("ch")
    z = lax.div(cx, 2)
    k = lax.rem(cx, 2)
    chip = x * Z + z

    def at(xx, zz, kk, yy):
        return (xx, zz * 2 + kk, yy)

    def xm(d):
        return lax.rem(x + d + X, X)

    def zm(d):
        return lax.rem(z + d + Z, Z)

    def ym(d):
        return lax.rem(y + d + Y, Y)

    sibling = at(x, z, 1 - k, y)
    x_to = {s: at(xm(s), z, k, y) for s in (1, -1, 2)}
    z_to = {s: at(x, zm(s), k, y) for s in (1, -1, 2, -2)}
    y_to = {s: at(x, z, k, ym(s)) for s in (1, -1)}

    offsets = sorted(
        ((dx, dz) for dx in range(X) for dz in range(Z) if dx or dz),
        key=lambda o: -min(o[0], X - o[0]) - min(o[1], Z - o[1]))

    barrier = pltpu.get_barrier_semaphore()
    x_across = {s: at(xm(s), z, 1 - k, y) for s in (1, -1, 2)}
    z_across = {s: at(x, zm(s), 1 - k, y) for s in (1, -1, 2, -2)}
    previous = lax.rem(chip + CHIPS - 1, CHIPS)
    greeted = [sibling, at(lax.div(previous, Z), lax.rem(previous, Z), 1 - k, y)]
    greeted += [at(x, z, k, ym(d)) for d in range(1, Y)]
    greeted += list(x_across.values()) + list(z_across.values())
    for target in greeted:
        pl.semaphore_signal(barrier, inc=1, device_id=target, device_id_type=MESH)

    for dx, dz in offsets:
        pl.semaphore_signal(barrier, inc=1, device_id=at(xm(dx), zm(dz), k, y), device_id_type=MESH)
    pl.semaphore_wait(barrier, CHIPS - 1 + len(greeted))

    arrivals, departures = {}, {}

    def send(name, src, dst, target, group):
        n = arrivals.setdefault(name, len(arrivals))
        g = departures.setdefault(group, len(departures))
        pltpu.make_async_remote_copy(
            src_ref=src, dst_ref=dst, send_sem=ss.at[g], recv_sem=rs.at[n],
            device_id=target, device_id_type=MESH).start()

    def recv(name, ref):
        pltpu.make_async_copy(ref, ref, rs.at[arrivals[name]]).wait()

    def sent(group, ref):
        pltpu.make_async_copy(ref, ref, ss.at[departures[group]]).wait()

    mine = pl.ds(pl.multiple_of(k * HALF, HALF), HALF)
    theirs = pl.ds(pl.multiple_of((1 - k) * HALF, HALF), HALF)

    own_rows = pl.ds(pl.multiple_of(chip * 128 + k * 64, 64), 64)
    sib_rows = pl.ds(pl.multiple_of(chip * 128 + (1 - k) * 64, 64), 64)
    my_lags = pl.ds(pl.multiple_of(k * ROWS, ROWS), ROWS)
    sib_lags = pl.ds(pl.multiple_of((1 - k) * ROWS, ROWS), ROWS)

    def tok_half(block, h):
        return tok.at[k, block, LEAD + h * 128:LEAD + (h + 1) * 128, :]

    def tok_all(half, block):
        return tok.at[half, block, LEAD:, :]

    quarter = pl.ds(pl.multiple_of(k * 256, 256), 256)
    nxt = lax.rem(chip + 1, CHIPS)

    def send_lead():
        @pl.when(k == 1)
        def _():
            for kk in (0, 1):
                cut = pl.ds(kk * 256, 256)
                send("lead", tokens.at[ROWS - LEAD:, cut], tok.at[0, y, 0:LEAD, cut],
                     at(lax.div(nxt, Z), lax.rem(nxt, Z), kk, y), "lead")

    def spread_lead():
        ref = tok.at[0, y, 0:LEAD, quarter]
        recv("lead", ref)
        for d in range(1, Y):
            send("leads", ref, ref, at(x, z, k, ym(d)), "leads")

    def share_lead():
        recv("leads", tok.at[0, 0:7, 0:LEAD, quarter])
        ref = tok.at[0, :, 0:LEAD, quarter]
        send("leadx", ref, ref, sibling, "leadx")

    def got_lead():
        recv("leadx", tok.at[0, :, 0:LEAD, quarter])

    both = (1, -1)
    side = {1: 0, -1: 1}

    def tok_recv(d, h):
        recv(("t", d, h), tok_all(0, 0))
        for s in (1, -1):
            block = ym(-s * d)
            half_block = tok_half(block, h)
            if d < 3:
                send(("t", d + 1, h), half_block, half_block, y_to[s], "t")
            elif h == side[s]:
                send(("t", 4), half_block, half_block, y_to[s], "t")
            if h == 1:
                send(("ts", d), tok_all(k, block), tok_all(k, block), sibling, "ts")

    def wrows(xx, zz, half=None):
        base = (xx * Z + zz) * 128
        if half is None:
            return pl.ds(pl.multiple_of(base, 128), 128)
        return pl.ds(pl.multiple_of(base + 64 * half, 64), 64)

    def hop(buf, name, xx, zz, target, half=None):
        ref = buf.at[wrows(xx, zz, half), :]
        send(name, ref, ref, target, "wq" if buf is wq else "wkv")

    def got(buf, name, blocks=2):
        recv(name, buf.at[0:128 * blocks, :])


    def first_hop(buf, name, steps, near, across):
        for s in steps:
            for columns, target in ((mine, near[s]), (theirs, across[s])):
                if buf is wq:
                    send(name, w_q.at[:, columns], wq.at[own_rows, :], target, "wq")
                else:
                    send(name, w_k.at[:, columns], wkv.at[own_rows, 0:HALF], target, "wkv")
                    send(name, w_v.at[:, columns], wkv.at[own_rows, HALF:2 * HALF], target, "wkv")

    def pass_ax():
        got(wq, "ax")
        for s in both:
            for b in both:
                hop(wq, ("az", 1, 1), xm(b), z, z_to[s])

    def pass_axx():
        got(wq, "axx", 1)
        for s in both:
            hop(wq, ("az", 2, 1), xm(2), z, z_to[s])

    def pass_az(b, d):
        columns = both if b == 1 else (b,)
        got(wq, ("az", b, d), 2 * len(columns))
        for col in columns:
            for s in both:
                hop(wq, ("az", b, d + 1), xm(col), zm(-s * d), z_to[s], side[s] if d == 3 else None)

    def pass_bz(d):
        got(wkv, ("bz", d))
        if d > 1:
            for s in both:
                hop(wkv, ("bz", d + 1), x, zm(-s * d), z_to[s], side[s] if d == 3 else None)
        for s in both:
            for m in (d, -d):
                hop(wkv, ("bx", d), x, zm(m), x_to[s])

    def pass_bz4():
        got(wkv, ("bz", 4), 1)
        for s in both:
            hop(wkv, ("bx", 4), x, zm(4), x_to[s])

    def pass_bx(d):
        rows = (0,) if d == 0 else (4,) if d == 4 else (d, -d)
        got(wkv, ("bx", d), 2 * len(rows))
        for m in rows:
            for s in both:
                hop(wkv, "bxx", xm(-s), zm(m), x_to[s], side[s])

    send_lead()
    for h in (0, 1):
        for s in (1, -1):
            send(("t", 1, h), tokens.at[h * 128:(h + 1) * 128, :], tok_half(y, h), y_to[s], "t")
    first_hop(wkv, ("bz", 1), both, z_to, z_across)
    first_hop(wq, "ax", both, x_to, x_across)
    first_hop(wkv, ("bz", 2), (2, -2), z_to, z_across)
    first_hop(wq, "axx", (2,), x_to, x_across)
    first_hop(wkv, ("bx", 0), both, x_to, x_across)
    first_hop(wq, ("az", 0, 1), both, z_to, z_across)
    send("sq", w_q.at[:, theirs], wq.at[own_rows, :], sibling, "sq")
    send("sk", w_k.at[:, theirs], wkv.at[own_rows, 0:HALF], sibling, "sk")
    send("sv", w_v.at[:, theirs], wkv.at[own_rows, HALF:2 * HALF], sibling, "sv")
    local = [
        pltpu.make_async_copy(w_q.at[:, mine], wq.at[own_rows, :], loc_sem.at[0]),
        pltpu.make_async_copy(w_k.at[:, mine], wkv.at[own_rows, 0:HALF], loc_sem.at[1]),
        pltpu.make_async_copy(w_v.at[:, mine], wkv.at[own_rows, HALF:2 * HALF], loc_sem.at[2]),
    ]
    for copy in local:
        copy.start()

    own_tok = pltpu.make_async_copy(tokens, tok_all(k, y), loc_sem.at[3])
    own_tok.start()
    send(("ts", 0), tokens, tok_all(k, y), sibling, "ts")
    send("f", filt.at[:, theirs], filt_s.at[my_lags, :], sibling, "f")
    own_filt = pltpu.make_async_copy(filt.at[:, mine], filt_s.at[my_lags, :], loc_sem.at[4])
    own_filt.start()
    own_taps = pltpu.make_async_copy(taps_hbm, taps_s, loc_sem.at[5])
    own_taps.start()
    own_bias = pltpu.make_async_copy(bias_hbm, bias_s, loc_sem.at[6])
    own_bias.start()


    def exchange(snd, rcv, n):
        for dx, dz in offsets:
            px, pz = xm(dx), zm(dz)
            pltpu.make_async_remote_copy(
                src_ref=snd.at[px * Z + pz], dst_ref=rcv.at[chip], send_sem=ss_x.at[n],
                recv_sem=rs_x.at[n], device_id=at(px, pz, k, y), device_id_type=MESH).start()
        rcv[chip] = snd[chip]

    def collect(rcv, n):
        all_but_one = rcv.at[0:CHIPS - 1]
        pltpu.make_async_copy(all_but_one, all_but_one, rs_x.at[n]).wait()

    def flushed(snd, n):
        all_but_one = snd.at[0:CHIPS - 1]
        pltpu.make_async_copy(all_but_one, all_but_one, ss_x.at[n]).wait()

    def send_filter():
        own_filt.wait()
        recv("f", filt_s.at[sib_lags, :])
        row_i = lax.broadcasted_iota(jnp.int32, (HALF, HALF), 0)
        col_i = lax.broadcasted_iota(jnp.int32, (HALF, HALF), 1)
        flip = (row_i + col_i == HALF - 1).astype(BF16)
        for jj in range(4):
            block = filt_s[jj * 128:(jj + 1) * 128, :].T.astype(BF16)
            stage[pl.ds(jj, HALF, stride=4), :] = jnp.dot(block, flip, preferred_element_type=F32)
        snd_h[...] = stage[...].astype(BF16).reshape(CHIPS, 16, HALF)
        exchange(snd_h, rcv_h, 0)

    def got_filter():
        collect(rcv_h, 0)
        flat[0:16, :] = jnp.zeros((16, HALF), F32)
        flat[16:, :] = rcv_h[...].astype(F32).reshape(CHIPS * 16, HALF)

    lane = lax.broadcasted_iota(jnp.int32, (BLK, HALF), 1)
    sub = lax.broadcasted_iota(jnp.int32, (BLK, HALF), 0)
    keep = lane + (BLK - 1) - sub < HALF

    def shifted_rows(c, v):
        j = 127 - v
        row = 16 + (j // 4) * 16 + 4 * c + j % 4
        wide = jnp.broadcast_to(flat[pl.ds(row, 1), :], (BLK, HALF))
        return pltpu.roll(wide, HALF - BLK + 1, 1, stride=1, stride_axis=0)

    def build(piece):
        c, first = piece // 2, piece % 2 * 8

        def body(d1, later):
            for p in range(7, -1, -1):
                now = shifted_rows(c, (15 - d1) * 8 + p)
                toep[c, d1, :, p * 128:(p + 1) * 128] = jnp.where(keep, now, later).astype(BF16)
                later = now
            return later

        carried = jnp.zeros((BLK, HALF), F32) if first == 0 else shifted_rows(c, (16 - first) * 8)
        lax.fori_loop(first, first + 8, body, carried)

    def project(block, half):
        rows = pl.ds(pl.multiple_of(block * KB, KB), KB)
        if half == 0:
            a, at_rows = tok[0, block], slice(0, LEAD + ROWS)
        else:
            a, at_rows = tok[1, block, LEAD:, :], slice(LEAD + ROWS, LEAD + POS)
        acc[at_rows, 0:HALF] += jnp.dot(a, wq[rows, :], preferred_element_type=F32)
        acc[at_rows, HALF:] += jnp.dot(a, wkv[rows, :], preferred_element_type=F32)

    far = ym(4)

    def project_column(first, count):
        def body(t, carry):
            block = 2 * xm(first + 2 * lax.div(t, 2)) + lax.rem(t, 2)

            @pl.when(block != far)
            def _():
                project(block, 0)
                project(block, 1)

            return carry

        lax.fori_loop(0, 2 * count, body, 0)

    acc[...] = jnp.zeros_like(acc)
    send_filter()
    spread_lead()
    pass_ax()
    pass_bz(1)
    tok_recv(1, 0)
    got(wq, "axx", 1)
    for s in both:
        hop(wq, ("az", 2, 1), xm(2), z, z_to[s])
    pass_bz(2)
    pass_bx(0)
    pass_az(0, 1)
    tok_recv(1, 1)
    pass_az(1, 1)
    pass_bx(1)
    pass_az(2, 1)
    tok_recv(2, 0)
    share_lead()
    pass_bx(2)
    pass_bz(3)
    pass_az(0, 2)
    got_filter()
    build(0)
    tok_recv(2, 1)
    pass_az(1, 2)
    build(1)
    pass_az(2, 2)
    pass_bz4()
    pass_az(0, 3)
    build(2)
    tok_recv(3, 0)
    pass_bx(3)
    pass_az(1, 3)
    build(3)
    pass_bx(4)
    pass_az(2, 3)
    tok_recv(3, 1)
    got(wq, ("az", 0, 4), 1)
    own_tok.wait()
    for copy in local:
        copy.wait()
    recv("sq", wq.at[sib_rows, :])
    recv("sk", wkv.at[sib_rows, 0:HALF])
    recv("sv", wkv.at[sib_rows, HALF:2 * HALF])
    got_lead()
    recv(("ts", 0), tok_all(0, 0))
    for d in (1, 2, 3):
        recv(("ts", d), tok.at[0, 0:2, LEAD:, :])
    project_column(0, 1)
    recv(("t", 4), tok_all(k, far))
    send(("ts", 4), tok_all(k, far), tok_all(k, far), sibling, "ts")
    got(wq, ("az", 1, 4), 2)
    project_column(1, 2)
    recv(("ts", 4), tok_all(0, 0))

    @pl.when(lax.div(far, 2) != xm(2))
    def _():
        project(far, 0)
        project(far, 1)

    got(wq, ("az", 2, 4), 1)
    got(wkv, "bxx", 8)

    def last_column(t, carry):
        block = 2 * xm(2) + t
        project(block, 0)
        project(block, 1)
        return carry

    lax.fori_loop(0, 2, last_column, 0)

    streams = (sq, sk, sv)

    def fill(i):
        streams[i][...] = acc[8:, i * HALF:(i + 1) * HALF].astype(BF16).astype(F32)

        @pl.when(chip == 0)
        def _():
            streams[i][0:8, :] = jnp.zeros((8, HALF), F32)

    fill(1)
    fill(2)
    own_taps.wait()
    own_bias.wait()

    def tap(i, j):
        return jnp.where(k == 0, taps_s[i, j:j + 1, 0:HALF], taps_s[i, j:j + 1, HALF:])

    def filtered(i, start, size):
        s = streams[i]
        return (tap(i, 0) * s[8 + start:8 + start + size, :] + tap(i, 1) * s[7 + start:7 + start + size, :]
                + tap(i, 2) * s[6 + start:6 + start + size, :])

    def gate(jj):
        block = filtered(1, jj * 128, 128) * filtered(2, jj * 128, 128)
        gated_s[jj * 128:(jj + 1) * 128, :] = block
        stage[pl.ds(jj, HALF, stride=4), :] = block.T

    for jj in range(4):
        gate(jj)
    snd_g[...] = stage[...].astype(BF16).reshape(CHIPS, 16, HALF)
    exchange(snd_g, rcv_g, 1)
    for piece in (4, 5, 6, 7):
        build(piece)
    fill(0)
    for jj in range(4):
        qconv_s[jj * 128:(jj + 1) * 128, :] = filtered(0, jj * 128, 128)
    collect(rcv_g, 1)

    flat[16:, :] = rcv_g[...].astype(F32).reshape(CHIPS * 16, HALF)
    epad[:, 0:16, :] = jnp.zeros((4, 16, HALF), F32)
    ysum[:, 0:16, :] = jnp.zeros((4, 16, HALF), F32)
    ysum[:, 16:, :] = jnp.zeros((4, 256, HALF), F32)
    low = lax.broadcasted_iota(jnp.int32, (CHIPS, HALF), 1) < BLK
    for c in range(4):
        for jj in range(4):
            now = flat[pl.ds(16 + 4 * c + jj, CHIPS, stride=16), :]
            prev_at = 16 + 4 * c + jj - 1 if jj else 4 * c + 3
            prev = flat[pl.ds(prev_at, CHIPS, stride=16), :]
            epad[c, pl.ds(16 + 2 * jj + 1, CHIPS, stride=8), :] = now
            epad[c, pl.ds(16 + 2 * jj, CHIPS, stride=8), :] = pltpu.roll(jnp.where(low, now, prev), BLK, 1)
        for p in range(8):
            windows[c, :, p * 128:(p + 1) * 128] = epad[c, 2 + 2 * p:2 + 2 * p + 256, :].astype(BF16)
        for u in range(4):
            count = 256 - 64 * u
            part = lax.dot_general(
                windows[c, 0:count, :], toep[c, 4 * u:4 * u + 4].reshape(4 * BLK, 1024),
                (((1,), (1,)), ((), ())), preferred_element_type=F32)
            for w in range(2):
                d = 64 * u + 32 * w
                ysum[c, 16 + d:, :] += part[0:256 - d, w * 128:(w + 1) * 128]
        for jj in range(4):
            a = ysum[c, pl.ds(16 + 2 * jj, CHIPS, stride=8), :]
            b = ysum[c, pl.ds(2 * jj, CHIPS, stride=8), :]
            e = ysum[c, pl.ds(16 + 2 * jj + 1, CHIPS, stride=8), :]
            f = ysum[c, pl.ds(2 * jj + 1, CHIPS, stride=8), :]
            stage[pl.ds(4 * c + jj, CHIPS, stride=16), :] = jnp.where(low, a, f) + pltpu.roll(
                jnp.where(low, e, b), BLK, 1)
    snd_y[...] = stage[...].astype(BF16).reshape(CHIPS, 16, HALF)
    exchange(snd_y, rcv_y, 2)
    collect(rcv_y, 2)

    stage[...] = rcv_y[...].astype(F32).reshape(CHIPS * 16, HALF)
    direct = jnp.where(k == 0, bias_s[:, 0:HALF], bias_s[:, HALF:])

    def mixed(jj):
        conv = stage[pl.ds(jj, HALF, stride=4), :].T
        at_rows = pl.ds(pl.multiple_of(jj * 128, 128), 128)
        return (qconv_s[at_rows, :] * (conv + direct * gated_s[at_rows, :])).astype(BF16)

    for t in (0, 1):
        obuf[t * 128:(t + 1) * 128, :] = mixed(2 * (1 - k) + t)
    send("o", obuf, out.at[:, mine], sibling, "o")
    for t in (0, 1):
        out[t * 128:(t + 1) * 128, mine] = mixed(2 * k + t)
    sent("sq", w_q.at[:, theirs])
    sent("sk", w_k.at[:, theirs])
    sent("sv", w_v.at[:, theirs])
    sent("f", filt.at[:, theirs])
    sent("t", tok.at[0, 0:7, LEAD:, :])
    sent("ts", tok.at[0, :, LEAD:, :])
    sent("wq", wq.at[0:31 * 128, :])
    sent("wkv", wkv.at[0:31 * 128, :])

    @pl.when(k == 1)
    def _():
        sent("lead", tokens.at[ROWS - LEAD:, :])

    sent("leads", tok.at[0, 0:7, 0:LEAD, quarter])
    sent("leadx", tok.at[0, :, 0:LEAD, quarter])
    for n, snd in enumerate((snd_h, snd_g, snd_y)):
        flushed(snd, n)
    sent("o", obuf)
    recv("o", out.at[:, theirs])


def on_device(tokens, w_query, w_key, w_value, short_taps, long_filter, filter_bias):
    hbm = pl.BlockSpec(memory_space=pltpu.HBM)
    dma = pltpu.SemaphoreType.DMA
    return pl.pallas_call(
        kernel,
        out_shape=jax.ShapeDtypeStruct((ROWS, 2 * HALF), BF16),
        in_specs=[hbm] * 7,
        out_specs=pl.BlockSpec(memory_space=pltpu.VMEM),
        scratch_shapes=[
            pltpu.VMEM((2, Y, LEAD + ROWS, KB), BF16),
            pltpu.VMEM((Y * KB, HALF), BF16),
            pltpu.VMEM((Y * KB, 2 * HALF), BF16),
            pltpu.VMEM((LEAD + POS, 3 * HALF), F32),
            pltpu.VMEM((POS + 8, HALF), F32),
            pltpu.VMEM((POS + 8, HALF), F32),
            pltpu.VMEM((POS + 8, HALF), F32),
            pltpu.VMEM((POS, HALF), F32),
            pltpu.VMEM((POS, HALF), F32),
            pltpu.VMEM((POS, HALF), F32),
            pltpu.VMEM((POS, HALF), F32),
            pltpu.VMEM((CHIPS, 16, HALF), BF16),
            pltpu.VMEM((CHIPS, 16, HALF), BF16),
            pltpu.VMEM((CHIPS, 16, HALF), BF16),
            pltpu.VMEM((CHIPS, 16, HALF), BF16),
            pltpu.VMEM((CHIPS, 16, HALF), BF16),
            pltpu.VMEM((CHIPS, 16, HALF), BF16),
            pltpu.VMEM((16 + POS, HALF), F32),
            pltpu.VMEM((4, 16 + 256, HALF), F32),
            pltpu.VMEM((4, 256, 1024), BF16),
            pltpu.VMEM((4, 16, BLK, 1024), BF16),
            pltpu.VMEM((4, 16 + 256, HALF), F32),
            pltpu.VMEM((ROWS, HALF), BF16),
            pltpu.VMEM((3, 3, 2 * HALF), F32),
            pltpu.VMEM((1, 2 * HALF), F32),
            dma((7,)),
            dma((N_SEND,)),
            dma((N_RECV,)),
            dma((3,)),
            dma((3,)),
        ],
        compiler_params=pltpu.CompilerParams(
            collective_id=0, has_side_effects=True, vmem_limit_bytes=61850 * 1024),
        name="hyena",
    )(tokens, w_query, w_key, w_value, short_taps, long_filter, filter_bias.reshape(1, -1))


def solution(mesh):
    return jax.shard_map(
        on_device,
        mesh=mesh,
        in_specs=(
            P(("fsdp", "ctx"), "ch"),
            P(("fsdp", "ctx"), "ch"),
            P(("fsdp", "ctx"), "ch"),
            P(("fsdp", "ctx"), "ch"),
            P(None, None, "ch"),
            P(("fsdp", "ctx"), "ch"),
            P("ch"),
        ),
        out_specs=P(("fsdp", "ctx"), "ch"),
        check_vma=False,
    )
```
